32 devices in a mesh: slab: 16 (over z, y, x), batch: 2 (over core).
Axes of the slice: x: 2, y: 2, z: 4, core: 2. Of those that a mesh axis runs over, the one named last changes fastest.
Arguments:
- field: bfloat16 [2, 16, 128, 256, 128], P('batch', None, 'slab'), may hold values from -6 to 6
- cotangent: bfloat16 [2, 16, 128, 256, 128], P('batch', None, 'slab'), may hold values from -6 to 6
- spectral_weight: bfloat16 [1024, 2, 16, 512], P('slab'), may hold values from -1 to 1
- point_weight: bfloat16 [16, 16], replicated, may hold values from -1.5 to 1.5
- point_bias: float32 [16], replicated, may hold values from -3 to 3
Outputs:
- input_grad: bfloat16 [2, 16, 128, 256, 128], P('batch', None, 'slab')
- grad_spec: float32 [1024, 2, 16, 512], P('slab')
- grad_point: float32 [16, 16], replicated
- grad_bias: float32 [16], replicated
The draws below stay inside these ranges and needn't reach their ends.
All inputs are finite; a program needn't handle non-finite values.
Results may differ from the reference program's by a relative error of at most 0.018.
Values may be sent and summed in bfloat16 or wider, within the bound.
A program may use at most 192 MiB of HBM per device.

```python
import math
import jax
import jax.numpy as jnp
from jax import lax

C = 16
MX = 32
MY = 32
MZ = 32
NY = 256
NZ = 128
CX = 8
NX = 128
PAIRS = 1024
SAMPLES = 2
N_SLAB = 16


def level_of(rng, extent, pieces, least, high):
    def one(dim, parts):
        draws = jax.random.uniform(jax.random.fold_in(jax.random.fold_in(rng, 6), dim), (parts,), jnp.float32, least / len(pieces), high / len(pieces))
        return jnp.repeat(jnp.exp(draws), extent[dim] // parts).reshape((-1,) + (1,) * (len(extent) - dim - 1))

    factor_of = one(*pieces[0])
    for cut in pieces[1:]:
        factor_of = factor_of * one(*cut)
    return factor_of


def gaussian(rng, shape, spread, bound, cuts=(), kind=jnp.bfloat16):
    values = jax.random.normal(rng, shape, jnp.float32) * spread
    if len(cuts) > 0:
        values = level_of(rng, shape, cuts, -0.22, 0.18) * values
    return jnp.clip(values, min=-bound, max=bound).astype(kind)


def setup_inputs(seed: int = 0) -> dict:
    keys = jax.random.split(jax.random.key(seed), 6)
    return {
        "field": gaussian(keys[0], (SAMPLES, C, NX, NY, NZ), 1.0, 6.0, ((0, 2), (2, 16))),
        "cotangent": gaussian(keys[1], (SAMPLES, C, NX, NY, NZ), 1.0, 6.0, ((0, 2), (2, 16))),
        "spectral_weight": gaussian(keys[2], (PAIRS, 2, C, C * MX), (2 * C) ** -0.5, 1.0, ((0, 16),)),
        "point_weight": gaussian(keys[3], (C, C), C ** -0.5, 1.5),
        "point_bias": gaussian(keys[4], (C,), 0.5, 3.0, (), jnp.float32),
    }


def float_einsum(form, left, right):
    return jnp.einsum(form, left.astype(jnp.float32), right.astype(jnp.float32), precision=lax.Precision.HIGHEST)

def mode_freqs(number, length):
    indices = jnp.arange(number, dtype=jnp.int32)
    return jnp.where(indices < number // 2, indices, indices + (length - number))

def phase_grid(positions, frequencies, length):
    product = positions[:, None] * frequencies[None, :] % length
    return product.astype(jnp.float32) * (2.0 * math.pi / length)

def rotation(phases, orient):
    cosine = jnp.cos(phases)
    sine_part = orient * jnp.sin(phases)
    upper = jnp.stack([cosine, -sine_part], axis=1)
    lower = jnp.stack([sine_part, cosine], axis=1)
    return jnp.stack([upper, lower], axis=0).astype(jnp.bfloat16)

def plane_tables(rows_y, rows_z):
    phase_y = phase_grid(jnp.arange(rows_y, dtype=jnp.int32), mode_freqs(MY, rows_y), rows_y)
    phase_z = phase_grid(jnp.arange(rows_z, dtype=jnp.int32), jnp.arange(MZ, dtype=jnp.int32), rows_z)
    forward_y = jnp.stack([jnp.cos(phase_y), -jnp.sin(phase_y)], axis=1).astype(jnp.bfloat16)
    forward_z = rotation(phase_z, 1.0)
    inverse_z = rotation(phase_z.T, -1.0)
    inverse_y = jnp.stack([jnp.cos(phase_y).T, -jnp.sin(phase_y).T], axis=0).astype(jnp.bfloat16)
    return (forward_y, forward_z, inverse_z, inverse_y)

def yz_forward(slab_data, tables):
    partial_value = float_einsum('bcxyz,yrm->bcxrmz', slab_data, tables[0]).astype(jnp.bfloat16)
    spectrum = float_einsum('bcxrmz,rzsk->bcxsmk', partial_value, tables[1]).astype(jnp.bfloat16)
    return spectrum.reshape(spectrum.shape[:4] + (MY * MZ,))

def yz_inverse(planes_in, tables, factor):
    shaped = planes_in.reshape(planes_in.shape[:4] + (MY, MZ))
    rolled = float_einsum('boxsmk,skrz->boxrmz', shaped, tables[2]).astype(jnp.bfloat16)
    return factor * float_einsum('boxrmz,rmy->boxyz', rolled, tables[3])

def x_forward(spectrum, table, factor):
    return factor * float_einsum('bcxrp,rxsa->bcsap', spectrum, table)

def x_inverse(spectrum, table):
    return float_einsum('bosap,sarx->boxrp', spectrum, table).astype(jnp.bfloat16)

def mix_modes(spectrum, weights_f):

    def apply(values, weight_part):
        return jnp.einsum('biap,pioa->boap', values, weight_part, precision=lax.Precision.HIGHEST)
    real_part, imag_part = (spectrum[:, :, 0], spectrum[:, :, 1])
    first = apply(real_part, weights_f[:, 0]) - apply(imag_part, weights_f[:, 1])
    second = apply(real_part, weights_f[:, 1]) + apply(imag_part, weights_f[:, 0])
    return jnp.stack([first, second], axis=2)

def adjoint_mix(spectrum, weights_f):

    def apply(values, weight_part):
        return jnp.einsum('boap,pioa->biap', values, weight_part, precision=lax.Precision.HIGHEST)
    real_part, imag_part = (spectrum[:, :, 0], spectrum[:, :, 1])
    first = apply(real_part, weights_f[:, 0]) + apply(imag_part, weights_f[:, 1])
    second = apply(imag_part, weights_f[:, 0]) - apply(real_part, weights_f[:, 1])
    return jnp.stack([first, second], axis=2)

def weight_grad(modes_in, modes_out):

    def apply(left, right):
        return jnp.einsum('biap,boap->pioa', left, right, precision=lax.Precision.HIGHEST)
    first = apply(modes_in[:, :, 0], modes_out[:, :, 0]) + apply(modes_in[:, :, 1], modes_out[:, :, 1])
    second = apply(modes_in[:, :, 0], modes_out[:, :, 1]) - apply(modes_in[:, :, 1], modes_out[:, :, 0])
    stacked = jnp.stack([first, second], axis=1)
    return stacked.reshape(stacked.shape[0], 2, stacked.shape[2], stacked.shape[3] * stacked.shape[4])

def activation_grad(pre, upstream):
    _, pull = jax.vjp(lambda values: jax.nn.gelu(values, approximate=True), pre)
    return pull(upstream)[0]

def split_blocks(array):
    shaped = array.reshape((array.shape[0], array.shape[1], N_SLAB, CX) + array.shape[3:])
    return jnp.moveaxis(shaped, 2, 0)

def join_blocks(array):
    moved = jnp.moveaxis(array, 0, 2)
    return moved.reshape((moved.shape[0], moved.shape[1], N_SLAB * CX) + moved.shape[4:])

def reference(field, cotangent, spectral_weight, point_weight, point_bias):
    tables = plane_tables(NY, NZ)
    phase_x = phase_grid(jnp.arange(NX, dtype=jnp.int32), mode_freqs(MX, NX), NX)
    forward_x = rotation(phase_x, 1.0)
    inverse_x = rotation(phase_x.T, -1.0)
    scale_f = 1.0 / math.sqrt(NX * NY * NZ)
    scale_i = 1.0 / math.sqrt(MX * MY * MZ)
    scale_p = 1.0 / math.sqrt(SAMPLES * NX * NY * NZ)
    scale_w = math.sqrt(MX * MY * MZ / (SAMPLES * NX * NY * NZ))
    weights_f = spectral_weight.astype(jnp.float32).reshape(PAIRS, 2, C, C, MX)
    field_blocks = split_blocks(field)
    cot_blocks = split_blocks(cotangent)
    planes_u = join_blocks(lax.map(lambda slab_data: yz_forward(slab_data, tables), field_blocks))
    modes_u = x_forward(planes_u, forward_x, scale_f)
    mixed = mix_modes(modes_u, weights_f).astype(jnp.bfloat16)
    back_v = split_blocks(x_inverse(mixed, inverse_x))

    def signal(field_part, cot_part, back_part):
        pre = yz_inverse(back_part, tables, scale_i) + float_einsum('bixyz,io->boxyz', field_part, point_weight)
        pre = pre + point_bias[None, :, None, None, None]
        return activation_grad(pre, cot_part.astype(jnp.float32)).astype(jnp.bfloat16)

    def first_pass(inputs):
        dpre = signal(inputs[0], inputs[1], inputs[2])
        point_part = float_einsum('bixyz,boxyz->io', inputs[0], dpre)
        bias_part = lax.optimization_barrier(jnp.sum(dpre.astype(jnp.float32), axis=(0, 2, 3, 4)))
        return (yz_forward(dpre, tables), point_part, bias_part)
    spec_blocks, point_parts, bias_parts = lax.map(first_pass, (field_blocks, cot_blocks, back_v))
    grad_point = scale_p * lax.optimization_barrier(jnp.sum(point_parts, axis=0))
    grad_bias = scale_p * lax.optimization_barrier(jnp.sum(bias_parts, axis=0))
    modes_d = x_forward(join_blocks(spec_blocks), forward_x, scale_i)
    grad_spec = scale_w * weight_grad(modes_u, modes_d)
    back_d = split_blocks(x_inverse(adjoint_mix(modes_d, weights_f).astype(jnp.bfloat16), inverse_x))

    def second_pass(inputs):
        dpre = signal(inputs[0], inputs[1], inputs[2])
        total = yz_inverse(inputs[3], tables, scale_f) + float_einsum('boxyz,io->bixyz', dpre, point_weight)
        return total.astype(jnp.bfloat16)
    input_grad = join_blocks(lax.map(second_pass, (field_blocks, cot_blocks, back_v, back_d)))
    return (input_grad, grad_spec, grad_point, grad_bias)
```

```python
import functools
import math

import jax
import jax.numpy as jnp
import ml_dtypes
import numpy as np
from jax import lax
from jax.experimental import pallas as pl
from jax.experimental.pallas import tpu as pltpu
from jax.sharding import PartitionSpec as P

MX = 32
MY = 32
MZ = 32
PB = 8
BF = jnp.bfloat16
F32 = jnp.float32
MESH = pl.DeviceIdType.MESH
VMEM = pl.BlockSpec(memory_space=pltpu.VMEM)


def np_freqs(number, length):
    indices = np.arange(number)
    return np.where(indices < number // 2, indices, indices + (length - number))


def np_phase(positions, frequencies, length):
    product = positions[:, None] * frequencies[None, :] % length
    return product.astype(np.float64) * (2.0 * math.pi / length)


def x_tables(n, planes, channels):
    total = n * planes
    phase = np_phase(np.arange(total), np_freqs(MX, total), total)
    cosine, sine = np.cos(phase), np.sin(phase)
    forward = np.stack(
        [np.stack([cosine, -sine], axis=1), np.stack([sine, cosine], axis=1)], axis=0
    )
    inverse = np.stack(
        [np.stack([cosine, -sine], axis=1), np.stack([sine, cosine], axis=1)], axis=0
    )

    def rows(table, copies):
        table = table.reshape(2, n, planes, 2, MX).transpose(1, 0, 2, 3, 4)
        table = table.reshape(n * 2 * planes, 2, 1, MX)
        table = np.broadcast_to(table, (table.shape[0], 2, copies, MX))
        return table.reshape(table.shape[0], 2 * copies * MX).astype(ml_dtypes.bfloat16)

    return jnp.asarray(rows(forward, channels)), jnp.asarray(rows(inverse, 4))


def enter(n, me, bat):
    barrier = pltpu.get_barrier_semaphore()

    def greet(k, carry):
        pl.semaphore_signal(
            barrier, inc=1, device_id={"slab": lax.rem(me + k, n)}, device_id_type=MESH
        )
        return carry

    lax.fori_loop(1, n, greet, 0)
    pl.semaphore_signal(barrier, inc=1, device_id={"batch": 1 - bat}, device_id_type=MESH)
    pl.semaphore_wait(barrier, n)


def peer_copy(n, me, k, source, target, landed, sems):
    to = lax.rem(me + k, n)
    return pltpu.make_async_remote_copy(
        src_ref=source(to),
        dst_ref=target(landed),
        send_sem=sems.at[0, k],
        recv_sem=sems.at[1, k],
        device_id={"slab": to},
        device_id_type=MESH,
    )


def send_all(n, me, source, target, sems):
    def step(k, carry):
        peer_copy(n, me, k, source, target, me, sems).start()
        return carry

    lax.fori_loop(1, n, step, 0)


def wait_all(n, me, source, target, sems):
    def step(k, carry):
        peer_copy(n, me, k, source, target, lax.rem(me - k + n, n), sems).wait()
        return carry

    lax.fori_loop(1, n, step, 0)


def expand(planes_ref, slot, block, table_ref):
    rows = planes_ref.shape[1] * planes_ref.shape[2]
    lanes = pl.ds(pl.multiple_of(block * (PB * 16), 128), PB * 16)
    part = planes_ref[slot, :, :, lanes].reshape(rows, PB * 16)
    both = lax.dot_general(
        part, table_ref[...], (((0,), (0,)), ((), ())), preferred_element_type=F32
    )
    half = both.shape[1] // 2
    return (
        both[:, :half].reshape(PB, 16, half),
        both[:, half:].reshape(PB, 16, half),
    )


def own_mask(channels):
    shape = (channels, channels * MX)
    row = lax.broadcasted_iota(jnp.int32, shape, 0)
    col = lax.broadcasted_iota(jnp.int32, shape, 1)
    low = row * MX
    return jnp.where((col >= low) & (col < low + MX), 1.0, 0.0).astype(F32)


def lane_fold(values):
    quarter = values.shape[-1] // 4
    return (
        values[..., :quarter]
        + values[..., quarter : 2 * quarter]
        + values[..., 2 * quarter : 3 * quarter]
        + values[..., 3 * quarter :]
    )


def contract(first, second, table_ref, out_ref, block):
    both = jnp.concatenate([lane_fold(first), lane_fold(second)], axis=-1)
    both = both.reshape(PB * 16, both.shape[-1]).astype(BF)
    result = lax.dot_general(
        table_ref[...], both, (((1,), (1,)), ((), ())), preferred_element_type=F32
    )
    lanes = pl.ds(pl.multiple_of(block * (PB * 16), 128), PB * 16)
    out_ref[:, :, lanes] = result.astype(BF).reshape(out_ref.shape[0], out_ref.shape[1], PB * 16)


def weight_pair(w_ref, block):
    at = pl.ds(block * PB, PB)
    return w_ref[at, 0].astype(F32), w_ref[at, 1].astype(F32)


def mix_forward(n, scale, s1, w, t, ti, r1, r2, s2, sems, pair):
    me = lax.axis_index("slab")
    bat = lax.axis_index("batch")
    enter(n, me, bat)
    one = (lambda to: s1.at[to], lambda at: r1.at[bat, at], sems.at[0])
    two = (lambda to: s2.at[to], lambda at: r2.at[at], sems.at[1])
    send_all(n, me, *one)
    r1[bat, me] = s1[me]
    wait_all(n, me, *one)
    cross = pltpu.make_async_remote_copy(
        src_ref=r1.at[bat],
        dst_ref=r1.at[bat],
        send_sem=pair.at[0],
        recv_sem=pair.at[1],
        device_id={"batch": 1 - bat},
        device_id_type=MESH,
    )
    cross.start()
    mask = own_mask(16)[None]

    def step(block, carry):
        u0, u1 = expand(r1, bat, block, t)
        u0, u1 = u0 * scale, u1 * scale
        w0, w1 = weight_pair(w, block)
        v0 = jnp.sum(u0 * w0 - u1 * w1, axis=1, keepdims=True) * mask
        v1 = jnp.sum(u0 * w1 + u1 * w0, axis=1, keepdims=True) * mask
        contract(v0, v1, ti, s2, block)
        return carry

    lax.fori_loop(0, w.shape[0] // PB, step, 0)
    send_all(n, me, *two)
    r2[me] = s2[me]
    cross.wait()
    wait_all(n, me, *two)


def mix_backward(
    n, scale_f, scale_i, scale_w, s3, part, w, t, ti, r1, grad, r4, total,
    r3, s4, slots, half, sems, pair,
):
    me = lax.axis_index("slab")
    bat = lax.axis_index("batch")
    enter(n, me, bat)
    one = (lambda to: s3.at[to], lambda at: r3.at[bat, at], sems.at[0])
    two = (lambda to: s4.at[to], lambda at: r4.at[at], sems.at[1])
    small = (lambda to: part, lambda at: slots.at[at], sems.at[2])
    send_all(n, me, *one)
    send_all(n, me, *small)
    r3[bat, me] = s3[me]
    slots[me] = part[...]
    wait_all(n, me, *one)

    def across(source, target, at):
        return pltpu.make_async_remote_copy(
            src_ref=source,
            dst_ref=target,
            send_sem=pair.at[2 * at],
            recv_sem=pair.at[2 * at + 1],
            device_id={"batch": 1 - bat},
            device_id_type=MESH,
        )

    cross = across(r3.at[bat], r3.at[bat], 0)
    cross.start()
    mask = own_mask(16)[None]

    def gradient(slot, block):
        d0, d1 = expand(r3, slot, block, t)
        d0 = jnp.sum(d0 * mask, axis=1, keepdims=True) * scale_i
        d1 = jnp.sum(d1 * mask, axis=1, keepdims=True) * scale_i
        return d0, d1

    def step(block, carry):
        d0, d1 = gradient(bat, block)
        w0, w1 = weight_pair(w, block)
        contract(d0 * w0 + d1 * w1, d1 * w0 - d0 * w1, ti, s4, block)
        return carry

    lax.fori_loop(0, w.shape[0] // PB, step, 0)
    send_all(n, me, *two)
    r4[me] = s4[me]
    wait_all(n, me, *small)
    summed = slots[0]
    for at in range(1, n):
        summed = summed + slots[at]
    half[bat] = summed
    other = across(half.at[bat], half.at[bat], 1)
    other.start()
    cross.wait()

    def outer(block, carry):
        at = pl.ds(block * PB, PB)
        first = None
        for slot in range(2):
            u0, u1 = expand(r1, slot, block, t)
            d0, d1 = gradient(slot, block)
            d0, d1 = d0 * (scale_f * scale_w), d1 * (scale_f * scale_w)
            real = u0 * d0 + u1 * d1
            imag = u0 * d1 - u1 * d0
            if first is None:
                first = (real, imag)
            else:
                grad[at, 0] = first[0] + real
                grad[at, 1] = first[1] + imag
        return carry

    lax.fori_loop(0, w.shape[0] // PB, outer, 0)
    other.wait()
    total[...] = half[0] + half[1]
    wait_all(n, me, *two)


def run_forward(n, scale, s1, w, t, ti):
    shape = jax.ShapeDtypeStruct
    return pl.pallas_call(
        functools.partial(mix_forward, n, scale),
        out_shape=(shape((2,) + s1.shape, BF), shape(s1.shape, BF)),
        in_specs=[VMEM] * 4,
        out_specs=(VMEM, VMEM),
        scratch_shapes=[
            pltpu.VMEM(s1.shape, BF),
            pltpu.SemaphoreType.DMA((2, 2, n)),
            pltpu.SemaphoreType.DMA((2,)),
        ],
        compiler_params=pltpu.CompilerParams(
            collective_id=0, has_side_effects=True, vmem_limit_bytes=40 << 20
        ),
        name="mix_forward",
    )(s1, w, t, ti)


def run_backward(n, scales, s3, part, w, t, ti, r1):
    shape = jax.ShapeDtypeStruct
    return pl.pallas_call(
        functools.partial(mix_backward, n, *scales),
        out_shape=(shape(w.shape, F32), shape(s3.shape, BF), shape(part.shape, F32)),
        in_specs=[VMEM] * 6,
        out_specs=(VMEM, VMEM, VMEM),
        scratch_shapes=[
            pltpu.VMEM((2,) + s3.shape, BF),
            pltpu.VMEM(s3.shape, BF),
            pltpu.VMEM((n,) + part.shape, F32),
            pltpu.VMEM((2,) + part.shape, F32),
            pltpu.SemaphoreType.DMA((3, 2, n)),
            pltpu.SemaphoreType.DMA((4,)),
        ],
        compiler_params=pltpu.CompilerParams(
            collective_id=1, has_side_effects=True, vmem_limit_bytes=48 << 20
        ),
        name="mix_backward",
    )(s3, part, w, t, ti, r1)

def half_einsum(form, left, right):
    return jnp.einsum(form, left, right, preferred_element_type=F32)


def plane_tables(rows_y, rows_z):
    phase_y = np_phase(np.arange(rows_y), np_freqs(MY, rows_y), rows_y)
    phase_z = np_phase(np.arange(rows_z), np.arange(MZ), rows_z)
    cy, sy, cz, sz = np.cos(phase_y), np.sin(phase_y), np.cos(phase_z), np.sin(phase_z)
    forward_y = np.stack([cy, -sy], axis=1)
    forward_z = np.stack([np.stack([cz, -sz], axis=1), np.stack([sz, cz], axis=1)], axis=0)
    cz, sz = cz.T, sz.T
    inverse_z = np.stack([np.stack([cz, sz], axis=1), np.stack([-sz, cz], axis=1)], axis=0)
    inverse_y = np.stack([cy.T, -sy.T], axis=0)
    return [jnp.asarray(v.astype(ml_dtypes.bfloat16)) for v in (forward_y, forward_z, inverse_z, inverse_y)]


def yz_forward(slab_data, tables):
    partial_value = half_einsum("cxyz,yrm->cxrmz", slab_data, tables[0]).astype(BF)
    return half_einsum("cxrmz,rzsk->cxsmk", partial_value, tables[1]).astype(BF)


def yz_inverse(shaped, tables, factor):
    rolled = half_einsum("oxsmk,skrz->oxrmz", shaped, tables[2]).astype(BF)
    return factor * half_einsum("oxrmz,rmy->oxyz", rolled, tables[3])


def activation_grad(pre, upstream):
    _, pull = jax.vjp(lambda values: jax.nn.gelu(values, approximate=True), pre)
    return pull(upstream)[0]


def to_send(spectrum, n):
    c, x, s, m, k = spectrum.shape
    parts = spectrum.reshape(c, x, s, n, (m * k) // n)
    return parts.transpose(3, 2, 1, 4, 0).reshape(n, s * x, (m * k) // n * c)


def from_received(received, planes, channels):
    n = received.shape[0]
    parts = received.reshape(n, 2, planes, -1, channels)
    return parts.transpose(4, 2, 1, 0, 3).reshape(channels, planes, 2, MY, MZ)


def body(field, cotangent, spectral_weight, point_weight, point_bias):
    samples, channels, planes, rows_y, rows_z = field.shape
    n = lax.axis_size("slab")
    total_samples = samples * lax.axis_size("batch")
    cells = n * planes * rows_y * rows_z
    scale_f = 1.0 / math.sqrt(cells)
    scale_i = 1.0 / math.sqrt(MX * MY * MZ)
    scale_p = 1.0 / math.sqrt(total_samples * cells)
    scale_w = math.sqrt(MX * MY * MZ / (total_samples * cells))
    tables = plane_tables(rows_y, rows_z)
    t, ti = x_tables(n, planes, channels)
    f = field[0]
    cot = cotangent[0]
    s1 = to_send(yz_forward(f, tables), n)
    r1, r2 = run_forward(n, scale_f, s1, spectral_weight, t, ti)
    back_v = from_received(r2, planes, channels)
    pre = yz_inverse(back_v, tables, scale_i) + half_einsum("ixyz,io->oxyz", f, point_weight)
    pre = pre + point_bias[:, None, None, None]
    dpre = activation_grad(pre, cot.astype(F32)).astype(BF)
    point_local = half_einsum("ixyz,oxyz->io", f, dpre)
    bias_local = jnp.sum(dpre.astype(F32), axis=(1, 2, 3))
    part = jnp.concatenate([point_local, bias_local[None], jnp.zeros((7, channels), F32)], axis=0)
    part = jnp.pad(part, ((0, 0), (0, 128 - channels)))
    s3 = to_send(yz_forward(dpre, tables), n)
    grad_spec, r4, total = run_backward(
        n, (scale_f, scale_i, scale_w), s3, part, spectral_weight, t, ti, r1
    )
    back_d = from_received(r4, planes, channels)
    input_grad = yz_inverse(back_d, tables, scale_f) + half_einsum(
        "oxyz,io->ixyz", dpre, point_weight
    )
    return (
        input_grad.astype(BF)[None],
        grad_spec,
        scale_p * total[:channels, :channels],
        scale_p * total[channels, :channels],
    )


def solution(mesh):
    placed = (
        P("batch", None, "slab", None, None),
        P("batch", None, "slab", None, None),
        P("slab", None, None, None),
        P(),
        P(),
    )
    return jax.shard_map(
        body,
        mesh=mesh,
        in_specs=placed,
        out_specs=(P("batch", None, "slab", None, None), P("slab", None, None, None), P(), P()),
        check_vma=False,
    )
```

```python
import functools
import math

import jax
import jax.numpy as jnp
import ml_dtypes
import numpy as np
from jax import lax
from jax.experimental import pallas as pl
from jax.experimental.pallas import tpu as pltpu
from jax.sharding import PartitionSpec as P

MX = 32
MY = 32
MZ = 32
PB = 16
BF = jnp.bfloat16
F32 = jnp.float32
MESH = pl.DeviceIdType.MESH
VMEM = pl.BlockSpec(memory_space=pltpu.VMEM)


def np_freqs(number, length):
    indices = np.arange(number)
    return np.where(indices < number // 2, indices, indices + (length - number))


def np_phase(positions, frequencies, length):
    product = positions[:, None] * frequencies[None, :] % length
    return product.astype(np.float64) * (2.0 * math.pi / length)


def x_tables(n, planes):
    total = n * planes
    phase = np_phase(np.arange(total), np_freqs(MX, total), total)
    cosine, sine = np.cos(phase), np.sin(phase)
    forward = np.stack(
        [np.stack([cosine, -sine], axis=1), np.stack([sine, cosine], axis=1)], axis=0
    )
    inverse = np.stack(
        [np.stack([cosine, -sine], axis=1), np.stack([sine, cosine], axis=1)], axis=0
    )

    def rows(table, copies):
        table = table.reshape(2, n, planes, 2, MX).transpose(1, 0, 2, 3, 4)
        table = table.reshape(n * 2 * planes, 2, 1, MX)
        table = np.broadcast_to(table, (table.shape[0], 2, copies, MX))
        return table.reshape(table.shape[0], 2 * copies * MX).astype(ml_dtypes.bfloat16)

    return jnp.asarray(rows(forward, 4)), jnp.asarray(rows(inverse, 4))


def enter(n, me, bat):
    barrier = pltpu.get_barrier_semaphore()

    def greet(k, carry):
        pl.semaphore_signal(
            barrier, inc=1, device_id={"slab": lax.rem(me + k, n)}, device_id_type=MESH
        )
        return carry

    lax.fori_loop(1, n, greet, 0)
    pl.semaphore_signal(barrier, inc=1, device_id={"batch": 1 - bat}, device_id_type=MESH)
    pl.semaphore_wait(barrier, n)


def peer_copy(n, me, k, source, target, landed, sems):
    to = lax.rem(me + k, n)
    return pltpu.make_async_remote_copy(
        src_ref=source(to),
        dst_ref=target(landed),
        send_sem=sems.at[0, k],
        recv_sem=sems.at[1, k],
        device_id={"slab": to},
        device_id_type=MESH,
    )


def send_all(n, me, source, target, sems):
    def step(k, carry):
        peer_copy(n, me, k, source, target, me, sems).start()
        return carry

    lax.fori_loop(1, n, step, 0)


def wait_all(n, me, source, target, sems):
    def step(k, carry):
        peer_copy(n, me, k, source, target, lax.rem(me - k + n, n), sems).wait()
        return carry

    lax.fori_loop(1, n, step, 0)


def in_halves(source, target, sems):
    lanes = source.shape[2] // 2
    return [
        (
            lambda to, at=pl.ds(h * lanes, lanes): source.at[to, :, at],
            lambda slot, at=pl.ds(h * lanes, lanes): target.at[slot, :, at],
            sems.at[h],
        )
        for h in range(2)
    ]


def block_pairs(count):
    return min(PB, count // 2)


def block_lanes(block, pairs):
    return pl.ds(pl.multiple_of(block * (pairs * 16), 128), pairs * 16)


def four(values):
    return jnp.concatenate([values] * 4, axis=-1)


def expand(planes_ref, slot, block, pairs, table_ref):
    rows = planes_ref.shape[1] * planes_ref.shape[2]
    part = planes_ref[slot, :, :, block_lanes(block, pairs)].reshape(rows, pairs * 16)
    both = lax.dot_general(
        part, table_ref[...], (((0,), (0,)), ((), ())), preferred_element_type=F32
    )
    half = both.shape[1] // 2
    return (
        both[:, :half].reshape(pairs, 16, half),
        both[:, half:].reshape(pairs, 16, half),
    )


def own_mask(channels):
    shape = (channels, channels * MX)
    row = lax.broadcasted_iota(jnp.int32, shape, 0)
    col = lax.broadcasted_iota(jnp.int32, shape, 1)
    low = row * MX
    return jnp.where((col >= low) & (col < low + MX), 1.0, 0.0).astype(F32)


def lane_fold(values):
    quarter = values.shape[-1] // 4
    return (
        values[..., :quarter]
        + values[..., quarter : 2 * quarter]
        + values[..., 2 * quarter : 3 * quarter]
        + values[..., 3 * quarter :]
    )


def contract(first, second, table_ref, out_ref, block, pairs):
    both = jnp.concatenate([lane_fold(first), lane_fold(second)], axis=-1)
    both = both.reshape(pairs * 16, both.shape[-1]).astype(BF)
    result = lax.dot_general(
        table_ref[...], both, (((1,), (1,)), ((), ())), preferred_element_type=F32
    )
    out_ref[:, :, block_lanes(block, pairs)] = result.astype(BF).reshape(
        out_ref.shape[0], out_ref.shape[1], pairs * 16
    )


def pair_places(count, block, pairs):
    wide = max(count // MZ, 1)
    deep = count // wide
    step = pairs // wide
    return [m * deep + block * step + k for k in range(step) for m in range(wide)]


def weight_pair(w_ref, block, pairs):
    places = pair_places(w_ref.shape[0], block, pairs)
    return tuple(
        jnp.stack([w_ref[at, part].astype(F32) for at in places], axis=0) for part in range(2)
    )


def mix_forward(n, scale, s1, w, t, ti, r1, r2, s2, sems, pair):
    me = lax.axis_index("slab")
    bat = lax.axis_index("batch")
    enter(n, me, bat)
    one = in_halves(s1, r1.at[bat], sems.at[0])
    two = in_halves(s2, r2, sems.at[1])
    pairs = block_pairs(w.shape[0])
    blocks = w.shape[0] // pairs // 2
    for h in range(2):
        send_all(n, me, *one[h])
    r1[bat, me] = s1[me]
    cross = pltpu.make_async_remote_copy(
        src_ref=r1.at[bat],
        dst_ref=r1.at[bat],
        send_sem=pair.at[0],
        recv_sem=pair.at[1],
        device_id={"batch": 1 - bat},
        device_id_type=MESH,
    )
    mask = own_mask(16)[None]

    def step(block, carry):
        u0, u1 = expand(r1, bat, block, pairs, t)
        u0, u1 = four(u0 * scale), four(u1 * scale)
        w0, w1 = weight_pair(w, block, pairs)
        v0 = jnp.sum(u0 * w0 - u1 * w1, axis=1, keepdims=True) * mask
        v1 = jnp.sum(u0 * w1 + u1 * w0, axis=1, keepdims=True) * mask
        contract(v0, v1, ti, s2, block, pairs)
        return carry

    for h in range(2):
        wait_all(n, me, *one[h])
        if h == 1:
            cross.start()
        lax.fori_loop(h * blocks, (h + 1) * blocks, step, 0)
        send_all(n, me, *two[h])
    r2[me] = s2[me]
    cross.wait()
    for h in range(2):
        wait_all(n, me, *two[h])


def mix_backward(
    n, scale_f, scale_i, scale_w, s3, part, w, t, ti, r1, grad, r4, total,
    r3, s4, slots, half, sems, pair,
):
    me = lax.axis_index("slab")
    bat = lax.axis_index("batch")
    enter(n, me, bat)
    one = in_halves(s3, r3.at[bat], sems.at[0])
    two = in_halves(s4, r4, sems.at[1])
    small = (lambda to: part, lambda at: slots.at[at], sems.at[2, 0])
    pairs = block_pairs(w.shape[0])
    blocks = w.shape[0] // pairs // 2
    send_all(n, me, *one[0])
    send_all(n, me, *one[1])
    send_all(n, me, *small)
    r3[bat, me] = s3[me]
    slots[me] = part[...]

    def across(source, target, at):
        return pltpu.make_async_remote_copy(
            src_ref=source,
            dst_ref=target,
            send_sem=pair.at[2 * at],
            recv_sem=pair.at[2 * at + 1],
            device_id={"batch": 1 - bat},
            device_id_type=MESH,
        )

    cross = across(r3.at[bat], r3.at[bat], 0)
    mask = own_mask(16)[None]

    def gradient(slot, block):
        d0, d1 = expand(r3, slot, block, pairs, t)
        d0, d1 = four(d0), four(d1)
        d0 = jnp.sum(d0 * mask, axis=1, keepdims=True) * scale_i
        d1 = jnp.sum(d1 * mask, axis=1, keepdims=True) * scale_i
        return d0, d1

    def step(block, carry):
        d0, d1 = gradient(bat, block)
        w0, w1 = weight_pair(w, block, pairs)
        contract(d0 * w0 + d1 * w1, d1 * w0 - d0 * w1, ti, s4, block, pairs)
        return carry

    for h in range(2):
        wait_all(n, me, *one[h])
        if h == 1:
            cross.start()
        lax.fori_loop(h * blocks, (h + 1) * blocks, step, 0)
        send_all(n, me, *two[h])
    r4[me] = s4[me]
    wait_all(n, me, *small)
    summed = slots[0]
    for at in range(1, n):
        summed = summed + slots[at]
    half[bat] = summed
    other = across(half.at[bat], half.at[bat], 1)
    other.start()
    cross.wait()

    def outer(block, carry):
        places = pair_places(w.shape[0], block, pairs)
        first = None
        for slot in range(2):
            u0, u1 = expand(r1, slot, block, pairs, t)
            u0, u1 = four(u0), four(u1)
            d0, d1 = gradient(slot, block)
            d0, d1 = d0 * (scale_f * scale_w), d1 * (scale_f * scale_w)
            real = u0 * d0 + u1 * d1
            imag = u0 * d1 - u1 * d0
            if first is None:
                first = (real, imag)
            else:
                real, imag = first[0] + real, first[1] + imag
                for row, at in enumerate(places):
                    grad[at, 0] = real[row]
                    grad[at, 1] = imag[row]
        return carry

    lax.fori_loop(0, 2 * blocks, outer, 0)
    other.wait()
    total[...] = half[0] + half[1]
    for h in range(2):
        wait_all(n, me, *two[h])


def run_forward(n, scale, s1, w, t, ti):
    shape = jax.ShapeDtypeStruct
    return pl.pallas_call(
        functools.partial(mix_forward, n, scale),
        out_shape=(shape((2,) + s1.shape, BF), shape(s1.shape, BF)),
        in_specs=[VMEM] * 4,
        out_specs=(VMEM, VMEM),
        scratch_shapes=[
            pltpu.VMEM(s1.shape, BF),
            pltpu.SemaphoreType.DMA((2, 2, 2, n)),
            pltpu.SemaphoreType.DMA((2,)),
        ],
        compiler_params=pltpu.CompilerParams(
            collective_id=0, has_side_effects=True, vmem_limit_bytes=40 << 20
        ),
        name="mix_forward",
    )(s1, w, t, ti)


def run_backward(n, scales, s3, part, w, t, ti, r1):
    shape = jax.ShapeDtypeStruct
    return pl.pallas_call(
        functools.partial(mix_backward, n, *scales),
        out_shape=(shape(w.shape, F32), shape(s3.shape, BF), shape(part.shape, F32)),
        in_specs=[VMEM] * 6,
        out_specs=(VMEM, VMEM, VMEM),
        scratch_shapes=[
            pltpu.VMEM((2,) + s3.shape, BF),
            pltpu.VMEM(s3.shape, BF),
            pltpu.VMEM((n,) + part.shape, F32),
            pltpu.VMEM((2,) + part.shape, F32),
            pltpu.SemaphoreType.DMA((3, 2, 2, n)),
            pltpu.SemaphoreType.DMA((4,)),
        ],
        compiler_params=pltpu.CompilerParams(
            collective_id=1, has_side_effects=True, vmem_limit_bytes=48 << 20
        ),
        name="mix_backward",
    )(s3, part, w, t, ti, r1)


def plane_tables(rows_y, rows_z):
    phase_y = np_phase(np.arange(rows_y), np_freqs(MY, rows_y), rows_y)
    phase_z = np_phase(np.arange(rows_z), np.arange(MZ), rows_z)
    cy, sy, cz, sz = np.cos(phase_y), np.sin(phase_y), np.cos(phase_z), np.sin(phase_z)
    forward_y = np.concatenate([cy, -sy], axis=1).T
    inverse_y = np.concatenate([cy, -sy], axis=1)
    forward_z = np.stack([np.stack([cz, -sz], axis=1), np.stack([sz, cz], axis=1)], axis=0)
    forward_z = forward_z.transpose(3, 2, 0, 1).reshape(2 * MZ, 2 * rows_z)
    cz, sz = cz.T, sz.T
    inverse_z = np.stack([np.stack([cz, sz], axis=1), np.stack([-sz, cz], axis=1)], axis=0)
    inverse_z = inverse_z.transpose(1, 0, 2, 3).reshape(2 * MZ, 2 * rows_z)
    return [
        jnp.asarray(v.astype(ml_dtypes.bfloat16))
        for v in (forward_y, forward_z, inverse_z, inverse_y)
    ]


def piece_layout(n):
    count = MY * MZ // n
    wide = max(count // MZ, 1)
    deep = count // wide
    return wide, deep, wide * 16


def pack_planes(acc, kbuf, out):
    planes, n = acc.shape[0], out.shape[0]
    wide, deep, width = piece_layout(n)
    for x in range(planes):
        for g in range(kbuf.shape[0]):
            kbuf[g, pl.ds(x, 2 * MZ, stride=planes), :] = acc[x, :, g * 128 : (g + 1) * 128]
    group = 128 // width
    for j in range(n):
        m0 = j * wide * deep // MZ
        k0 = j * wide * deep % MZ if wide == 1 else 0
        for first in range(0, deep, group):
            parts = [
                kbuf[
                    m0 * 16 // 128,
                    (k0 + first + q) * 2 * planes : (k0 + first + q + 1) * 2 * planes,
                    m0 * 16 % 128 : m0 * 16 % 128 + width,
                ]
                for q in range(group)
            ]
            out[j, :, first * width : first * width + 128] = jnp.concatenate(
                parts, axis=1
            ).astype(BF)


def unpack_planes(received, kbuf, staged):
    planes, n = staged.shape[0], received.shape[0]
    wide, deep, width = piece_layout(n)
    group = 128 // width
    for k in range(MZ):
        owners = [j for j in range(n) if wide > 1 or j % (MZ // deep) == k // deep]
        lane = (k % deep) * width
        low = lane // 128 * 128
        for first in range(0, len(owners), group):
            parts = [
                received[j, :, low : low + 128].astype(F32)[:, lane - low : lane - low + width]
                for j in owners[first : first + group]
            ]
            kbuf[first // group, k * 2 * planes : (k + 1) * 2 * planes, :] = jnp.concatenate(
                parts, axis=1
            )
    for x in range(planes):
        for g in range(kbuf.shape[0]):
            staged[x, :, g * 128 : (g + 1) * 128] = kbuf[
                g, pl.ds(x, 2 * MZ, stride=planes), :
            ].astype(BF)


def plane_forward(source, fy, fz, lines, acc, x):
    channels = source.shape[0]
    rows = 2 * MY
    for c in range(channels):
        lines[pl.ds(c, rows, stride=channels), :] = jnp.dot(
            fy[...], source[c, 0], preferred_element_type=F32
        )
    half = MY * channels
    both = jnp.concatenate([lines[:half].astype(BF), lines[half:].astype(BF)], axis=1)
    acc[x] = lax.dot_general(fz[...], both, (((1,), (1,)), ((), ())), preferred_element_type=F32)


def spread_map(weight, spread, turned):
    size = spread.shape[0]
    place = lax.broadcasted_iota(jnp.int32, (size, weight.shape[0]), 0) >> 4
    lane = lax.broadcasted_iota(jnp.int32, (size, weight.shape[0]), 1)
    copies = jnp.where(place == lane, 1.0, 0.0).astype(BF)
    contracted = 0 if turned else 1
    rows = lax.dot_general(
        copies, weight[...], (((1,), (contracted,)), ((), ())), preferred_element_type=F32
    ).astype(BF)
    full = lax.dot_general(rows, copies, (((1,), (1,)), ((), ())), preferred_element_type=F32)
    row = lax.broadcasted_iota(jnp.int32, (size, size), 0)
    col = lax.broadcasted_iota(jnp.int32, (size, size), 1)
    spread[...] = jnp.where((row & 15) == (col & 15), full, 0.0).astype(BF)


def plane_inverse(staged, iz, iy, factor, lines, pre, x):
    channels = pre.shape[0]
    half = MY * channels
    rolled = factor * lax.dot_general(
        staged[x], iz[...], (((0,), (0,)), ((), ())), preferred_element_type=F32
    )
    lines[:half] = rolled[:, : rolled.shape[1] // 2]
    lines[half:] = rolled[:, rolled.shape[1] // 2 :]
    for c in range(0, channels, 2):
        pieces = []
        for at in (c, c + 1):
            pieces.append(lines[pl.ds(at, 2 * MY, stride=channels), :].astype(BF))
        result = jnp.dot(
            iy[...], jnp.concatenate(pieces, axis=1), preferred_element_type=F32
        )
        pre[c] = result[:, : result.shape[1] // 2]
        pre[c + 1] = result[:, result.shape[1] // 2 :]


def field_forward(field, fy, fz, out, lines, acc, kbuf):
    x = pl.program_id(0)
    plane_forward(field, fy, fz, lines, acc, x)

    @pl.when(x == pl.num_programs(0) - 1)
    def _():
        pack_planes(acc, kbuf, out)


def tile_rows(ref, step):
    parts = []
    for half in range(2):
        at = slice((2 * step + half) * 16, (2 * step + half + 1) * 16)
        value = ref[:, 0, at, :]
        parts.append(value.reshape(value.shape[0] * 16, value.shape[2]))
    return jnp.concatenate(parts, axis=1)


GELU_K = math.sqrt(2.0 / math.pi)
GELU_C = 0.044715


def gelu_slope(value):
    square = value * value
    bent = jnp.tanh(value * (GELU_K + (GELU_K * GELU_C) * square))
    side = value * (0.5 * GELU_K + (1.5 * GELU_K * GELU_C) * square)
    return (1.0 + bent) * (0.5 + (1.0 - bent) * side)


def middle(
    factor, received, field, cot, weight, bias, fy, fz, iz, iy,
    dpre, out, part, lines, acc, kbuf, staged, pre, spread, outer, sums,
):
    x = pl.program_id(0)
    channels = field.shape[0]

    @pl.when(x == 0)
    def _():
        unpack_planes(received, kbuf, staged)
        spread_map(weight, spread, False)
        outer[...] = jnp.zeros_like(outer)
        sums[...] = jnp.zeros_like(sums)

    plane_inverse(staged, iz, iy, factor, lines, pre, x)

    for at in range(field.shape[2] // 32):
        tile = tile_rows(field, at)
        mixed = jnp.dot(spread[...], tile, preferred_element_type=F32)
        width = mixed.shape[1] // 2
        halves = []
        for half in range(2):
            rows = slice((2 * at + half) * 16, (2 * at + half + 1) * 16)
            value = mixed[:, half * width : (half + 1) * width].reshape(channels, 16, width)
            value = value + pre[:, rows, :] + bias[...][:, None, :]
            slope = gelu_slope(value) * cot[:, 0, rows, :].astype(F32)
            rounded = slope.astype(BF)
            dpre[:, 0, rows, :] = rounded
            wide = rounded.astype(F32)
            sums[...] += wide[:, :8] + wide[:, 8:]
            halves.append(rounded.reshape(channels * 16, width))
        outer[...] += lax.dot_general(
            tile, jnp.concatenate(halves, axis=1), (((1,), (1,)), ((), ())),
            preferred_element_type=F32,
        )
    plane_forward(dpre, fy, fz, lines, acc, x)

    @pl.when(x == pl.num_programs(0) - 1)
    def _():
        pack_planes(acc, kbuf, out)
        size = channels * 16
        row = lax.broadcasted_iota(jnp.int32, (size, size), 0)
        col = lax.broadcasted_iota(jnp.int32, (size, size), 1)
        kept = jnp.where((row & 15) == (col & 15), outer[...], 0.0)
        kept = jnp.sum(kept.reshape(channels, 16, size), axis=1)
        place = lax.broadcasted_iota(jnp.int32, (size, 128), 0) >> 4
        lane = lax.broadcasted_iota(jnp.int32, (size, 128), 1)
        gather = jnp.where(place == lane, 1.0, 0.0).astype(F32)
        part[:channels] = jnp.dot(
            kept, gather, preferred_element_type=F32, precision=lax.Precision.HIGHEST
        )
        part[channels:] = jnp.sum(sums[...], axis=1)


def last(factor, received, dpre, weight, iz, iy, grad, lines, kbuf, staged, pre, spread):
    x = pl.program_id(0)
    channels = dpre.shape[0]

    @pl.when(x == 0)
    def _():
        unpack_planes(received, kbuf, staged)
        spread_map(weight, spread, True)

    plane_inverse(staged, iz, iy, factor, lines, pre, x)

    for at in range(dpre.shape[2] // 32):
        mixed = jnp.dot(spread[...], tile_rows(dpre, at), preferred_element_type=F32)
        width = mixed.shape[1] // 2
        for half in range(2):
            rows = slice((2 * at + half) * 16, (2 * at + half + 1) * 16)
            value = mixed[:, half * width : (half + 1) * width].reshape(channels, 16, width)
            grad[:, 0, rows, :] = (value + pre[:, rows, :]).astype(BF)


def whole(array):
    zeros = (0,) * array.ndim
    return pl.BlockSpec(array.shape, lambda x: zeros)


def plane_block(array):
    c, _, y, z = array.shape
    return pl.BlockSpec((c, 1, y, z), lambda x: (0, x, 0, 0))


def scratch(field, *names):
    c, planes, y, z = field.shape
    every = {
        "lines": pltpu.VMEM((2 * MY * c, z), F32),
        "acc": pltpu.VMEM((planes, 2 * MZ, MY * c), F32),
        "kbuf": pltpu.VMEM((MY * c // 128, 2 * MZ * planes, 128), F32),
        "staged": pltpu.VMEM((planes, 2 * MZ, MY * c), BF),
        "pre": pltpu.VMEM((c, y, z), F32),
        "spread": pltpu.VMEM((16 * c, 16 * c), BF),
        "outer": pltpu.VMEM((16 * c, 16 * c), F32),
        "sums": pltpu.VMEM((c, 8, z), F32),
    }
    return [every[name] for name in names]


def params():
    return pltpu.CompilerParams(vmem_limit_bytes=48 << 20)


def run_first(n, field, fy, fz):
    c, planes, _, _ = field.shape
    out = jax.ShapeDtypeStruct((n, 2 * planes, MY * MZ // n * c), BF)
    return pl.pallas_call(
        field_forward,
        grid=(planes,),
        out_shape=out,
        in_specs=[plane_block(field), whole(fy), whole(fz)],
        out_specs=whole(out),
        scratch_shapes=scratch(field, "lines", "acc", "kbuf"),
        compiler_params=params(),
        name="field_forward",
    )(field, fy, fz)


def run_middle(factor, received, field, cot, weight, bias, fy, fz, iz, iy):
    c, planes, _, _ = field.shape
    out = jax.ShapeDtypeStruct(received.shape, BF)
    part = jax.ShapeDtypeStruct((2 * c, 128), F32)
    flat = [weight, bias, fy, fz, iz, iy]
    return pl.pallas_call(
        functools.partial(middle, factor),
        grid=(planes,),
        out_shape=(jax.ShapeDtypeStruct(field.shape, BF), out, part),
        in_specs=[whole(received), plane_block(field), plane_block(cot)] + [whole(v) for v in flat],
        out_specs=(plane_block(field), whole(out), whole(part)),
        scratch_shapes=scratch(
            field, "lines", "acc", "kbuf", "staged", "pre", "spread", "outer", "sums"
        ),
        compiler_params=params(),
        name="middle",
    )(received, field, cot, *flat)


def run_last(factor, received, dpre, weight, iz, iy):
    c, planes, _, _ = dpre.shape
    flat = [weight, iz, iy]
    return pl.pallas_call(
        functools.partial(last, factor),
        grid=(planes,),
        out_shape=jax.ShapeDtypeStruct(dpre.shape, BF),
        in_specs=[whole(received), plane_block(dpre)] + [whole(v) for v in flat],
        out_specs=plane_block(dpre),
        scratch_shapes=scratch(dpre, "lines", "kbuf", "staged", "pre", "spread"),
        compiler_params=params(),
        name="last",
    )(received, dpre, *flat)


def body(field, cotangent, spectral_weight, point_weight, point_bias):
    samples, channels, planes, rows_y, rows_z = field.shape
    n = lax.axis_size("slab")
    total_samples = samples * lax.axis_size("batch")
    cells = n * planes * rows_y * rows_z
    scale_f = 1.0 / math.sqrt(cells)
    scale_i = 1.0 / math.sqrt(MX * MY * MZ)
    scale_p = 1.0 / math.sqrt(total_samples * cells)
    scale_w = math.sqrt(MX * MY * MZ / (total_samples * cells))
    fy, fz, iz, iy = plane_tables(rows_y, rows_z)
    t, ti = x_tables(n, planes)
    f = field.reshape(field.shape[1:])
    cot = cotangent.reshape(cotangent.shape[1:])
    s1 = run_first(n, f, fy, fz)
    r1, r2 = run_forward(n, scale_f, s1, spectral_weight, t, ti)
    bias = point_bias[:, None]
    dpre, s3, part = run_middle(
        scale_i, r2, f, cot, point_weight, bias, fy, fz, iz, iy
    )
    grad_spec, r4, total = run_backward(
        n, (scale_f, scale_i, scale_w), s3, part, spectral_weight, t, ti, r1
    )
    input_grad = run_last(scale_f, r4, dpre, point_weight, iz, iy)
    return (
        input_grad[None],
        grad_spec,
        scale_p * total[:channels, :channels],
        scale_p * jnp.sum(total[channels:], axis=1),
    )


def solution(mesh):
    placed = (
        P("batch", None, "slab", None, None),
        P("batch", None, "slab", None, None),
        P("slab", None, None, None),
        P(),
        P(),
    )
    return jax.shard_map(
        body,
        mesh=mesh,
        in_specs=placed,
        out_specs=(P("batch", None, "slab", None, None), P("slab", None, None, None), P(), P()),
        check_vma=False,
    )
```

```python
import functools
import math

import jax
import jax.numpy as jnp
import ml_dtypes
import numpy as np
from jax import lax
from jax.experimental import pallas as pl
from jax.experimental.pallas import tpu as pltpu
from jax.sharding import PartitionSpec as P

MX = 32
MY = 32
MZ = 32
PB = 16
BF = jnp.bfloat16
F32 = jnp.float32
MESH = pl.DeviceIdType.MESH
VMEM = pl.BlockSpec(memory_space=pltpu.VMEM)


def np_freqs(number, length):
    indices = np.arange(number)
    return np.where(indices < number // 2, indices, indices + (length - number))


def np_phase(positions, frequencies, length):
    product = positions[:, None] * frequencies[None, :] % length
    return product.astype(np.float64) * (2.0 * math.pi / length)


def x_tables(n, planes):
    total = n * planes
    phase = np_phase(np.arange(total), np_freqs(MX, total), total)
    cosine, sine = np.cos(phase), np.sin(phase)
    forward = np.stack(
        [np.stack([cosine, -sine], axis=1), np.stack([sine, cosine], axis=1)], axis=0
    )
    inverse = np.stack(
        [np.stack([cosine, -sine], axis=1), np.stack([sine, cosine], axis=1)], axis=0
    )

    def rows(table, copies):
        table = table.reshape(2, n, planes, 2, MX).transpose(1, 0, 2, 3, 4)
        table = table.reshape(n * 2 * planes, 2, 1, MX)
        table = np.broadcast_to(table, (table.shape[0], 2, copies, MX))
        return table.reshape(table.shape[0], 2 * copies * MX).astype(ml_dtypes.bfloat16)

    return jnp.asarray(rows(forward, 4)), jnp.asarray(rows(inverse, 4))


def enter(n, me, bat):
    barrier = pltpu.get_barrier_semaphore()

    def greet(k, carry):
        pl.semaphore_signal(
            barrier, inc=1, device_id={"slab": lax.rem(me + k, n)}, device_id_type=MESH
        )
        return carry

    lax.fori_loop(1, n, greet, 0)
    pl.semaphore_signal(barrier, inc=1, device_id={"batch": 1 - bat}, device_id_type=MESH)
    pl.semaphore_wait(barrier, n)


def peer_copy(n, me, k, source, target, landed, sems):
    to = lax.rem(me + k, n)
    return pltpu.make_async_remote_copy(
        src_ref=source(to),
        dst_ref=target(landed),
        send_sem=sems.at[0, k],
        recv_sem=sems.at[1, k],
        device_id={"slab": to},
        device_id_type=MESH,
    )


def send_all(n, me, source, target, sems):
    def step(i, carry):
        k = n // 2 + (i + 1) // 2 * (2 * (i % 2) - 1)
        peer_copy(n, me, k, source, target, me, sems).start()
        return carry

    lax.fori_loop(0, n - 1, step, 0)


def wait_all(n, me, source, target, sems):
    def step(k, carry):
        peer_copy(n, me, k, source, target, lax.rem(me - k + n, n), sems).wait()
        return carry

    lax.fori_loop(1, n, step, 0)


def in_halves(source, target, sems):
    lanes = source.shape[2] // 2
    return [
        (
            lambda to, at=pl.ds(h * lanes, lanes): source.at[to, :, at],
            lambda slot, at=pl.ds(h * lanes, lanes): target.at[slot, :, at],
            sems.at[h],
        )
        for h in range(2)
    ]


def block_pairs(count):
    return min(PB, count // 2)


def block_lanes(block, pairs):
    return pl.ds(pl.multiple_of(block * (pairs * 16), 128), pairs * 16)


def four(values):
    return jnp.concatenate([values] * 4, axis=-1)


def expand(planes_ref, slot, block, pairs, table_ref):
    rows = planes_ref.shape[1] * planes_ref.shape[2]
    part = planes_ref[slot, :, :, block_lanes(block, pairs)].reshape(rows, pairs * 16)
    both = lax.dot_general(
        part, table_ref[...], (((0,), (0,)), ((), ())), preferred_element_type=F32
    )
    half = both.shape[1] // 2
    return (
        both[:, :half].reshape(pairs, 16, half),
        both[:, half:].reshape(pairs, 16, half),
    )


def own_mask(channels):
    shape = (channels, channels * MX)
    row = lax.broadcasted_iota(jnp.int32, shape, 0)
    col = lax.broadcasted_iota(jnp.int32, shape, 1)
    low = row * MX
    return jnp.where((col >= low) & (col < low + MX), 1.0, 0.0).astype(F32)


def lane_fold(values):
    quarter = values.shape[-1] // 4
    return (
        values[..., :quarter]
        + values[..., quarter : 2 * quarter]
        + values[..., 2 * quarter : 3 * quarter]
        + values[..., 3 * quarter :]
    )


def contract(first, second, table_ref, out_ref, block, pairs):
    both = jnp.concatenate([lane_fold(first), lane_fold(second)], axis=-1)
    both = both.reshape(pairs * 16, both.shape[-1]).astype(BF)
    result = lax.dot_general(
        table_ref[...], both, (((1,), (1,)), ((), ())), preferred_element_type=F32
    )
    out_ref[:, :, block_lanes(block, pairs)] = result.astype(BF).reshape(
        out_ref.shape[0], out_ref.shape[1], pairs * 16
    )


def pair_places(count, block, pairs):
    wide = max(count // MZ, 1)
    deep = count // wide
    step = pairs // wide
    return [m * deep + block * step + k for k in range(step) for m in range(wide)]


def weight_pair(w_ref, block, pairs):
    places = pair_places(w_ref.shape[0], block, pairs)
    return tuple(
        jnp.stack([w_ref[at, part].astype(F32) for at in places], axis=0) for part in range(2)
    )


def mix_forward(n, scale, s1, w, t, ti, r1, r2, s2, sems, pair):
    me = lax.axis_index("slab")
    bat = lax.axis_index("batch")
    enter(n, me, bat)
    one = in_halves(s1, r1.at[bat], sems.at[0])
    two = in_halves(s2, r2, sems.at[1])
    pairs = block_pairs(w.shape[0])
    blocks = w.shape[0] // pairs // 2
    for h in range(2):
        send_all(n, me, *one[h])
    r1[bat, me] = s1[me]
    cross = pltpu.make_async_remote_copy(
        src_ref=r1.at[bat],
        dst_ref=r1.at[bat],
        send_sem=pair.at[0],
        recv_sem=pair.at[1],
        device_id={"batch": 1 - bat},
        device_id_type=MESH,
    )
    mask = own_mask(16)[None]

    def step(block, carry):
        u0, u1 = expand(r1, bat, block, pairs, t)
        u0, u1 = four(u0 * scale), four(u1 * scale)
        w0, w1 = weight_pair(w, block, pairs)
        v0 = jnp.sum(u0 * w0 - u1 * w1, axis=1, keepdims=True) * mask
        v1 = jnp.sum(u0 * w1 + u1 * w0, axis=1, keepdims=True) * mask
        contract(v0, v1, ti, s2, block, pairs)
        return carry

    for h in range(2):
        wait_all(n, me, *one[h])
        if h == 1:
            cross.start()
        lax.fori_loop(h * blocks, (h + 1) * blocks, step, 0)
        send_all(n, me, *two[h])
    r2[me] = s2[me]
    cross.wait()
    for h in range(2):
        wait_all(n, me, *two[h])


def mix_backward(
    n, scale_f, scale_i, scale_w, s3, part, w, t, ti, r1, grad, r4, total,
    r3, s4, slots, half, sems, pair,
):
    me = lax.axis_index("slab")
    bat = lax.axis_index("batch")
    enter(n, me, bat)
    one = in_halves(s3, r3.at[bat], sems.at[0])
    two = in_halves(s4, r4, sems.at[1])
    small = (lambda to: part, lambda at: slots.at[at], sems.at[2, 0])
    pairs = block_pairs(w.shape[0])
    blocks = w.shape[0] // pairs // 2
    send_all(n, me, *one[0])
    send_all(n, me, *one[1])
    send_all(n, me, *small)
    r3[bat, me] = s3[me]
    slots[me] = part[...]

    def across(source, target, at):
        return pltpu.make_async_remote_copy(
            src_ref=source,
            dst_ref=target,
            send_sem=pair.at[2 * at],
            recv_sem=pair.at[2 * at + 1],
            device_id={"batch": 1 - bat},
            device_id_type=MESH,
        )

    cross = across(r3.at[bat], r3.at[bat], 0)
    mask = own_mask(16)[None]

    def gradient(slot, block):
        d0, d1 = expand(r3, slot, block, pairs, t)
        d0, d1 = four(d0), four(d1)
        d0 = jnp.sum(d0 * mask, axis=1, keepdims=True) * scale_i
        d1 = jnp.sum(d1 * mask, axis=1, keepdims=True) * scale_i
        return d0, d1

    def step(block, carry):
        d0, d1 = gradient(bat, block)
        w0, w1 = weight_pair(w, block, pairs)
        contract(d0 * w0 + d1 * w1, d1 * w0 - d0 * w1, ti, s4, block, pairs)
        return carry

    for h in range(2):
        wait_all(n, me, *one[h])
        if h == 1:
            cross.start()
        lax.fori_loop(h * blocks, (h + 1) * blocks, step, 0)
        send_all(n, me, *two[h])
    r4[me] = s4[me]
    wait_all(n, me, *small)
    summed = slots[0]
    for at in range(1, n):
        summed = summed + slots[at]
    half[bat] = summed
    other = across(half.at[bat], half.at[bat], 1)
    other.start()
    cross.wait()

    def outer(block, carry):
        places = pair_places(w.shape[0], block, pairs)
        first = None
        for slot in range(2):
            u0, u1 = expand(r1, slot, block, pairs, t)
            u0, u1 = four(u0), four(u1)
            d0, d1 = gradient(slot, block)
            d0, d1 = d0 * (scale_f * scale_w), d1 * (scale_f * scale_w)
            real = u0 * d0 + u1 * d1
            imag = u0 * d1 - u1 * d0
            if first is None:
                first = (real, imag)
            else:
                real, imag = first[0] + real, first[1] + imag
                for row, at in enumerate(places):
                    grad[at, 0] = real[row]
                    grad[at, 1] = imag[row]
        return carry

    lax.fori_loop(0, 2 * blocks, outer, 0)
    other.wait()
    total[...] = half[0] + half[1]
    for h in range(2):
        wait_all(n, me, *two[h])


def run_forward(n, scale, s1, w, t, ti):
    shape = jax.ShapeDtypeStruct
    return pl.pallas_call(
        functools.partial(mix_forward, n, scale),
        out_shape=(shape((2,) + s1.shape, BF), shape(s1.shape, BF)),
        in_specs=[VMEM] * 4,
        out_specs=(VMEM, VMEM),
        scratch_shapes=[
            pltpu.VMEM(s1.shape, BF),
            pltpu.SemaphoreType.DMA((2, 2, 2, n)),
            pltpu.SemaphoreType.DMA((2,)),
        ],
        compiler_params=pltpu.CompilerParams(
            collective_id=0, has_side_effects=True, vmem_limit_bytes=40 << 20
        ),
        name="mix_forward",
    )(s1, w, t, ti)


def run_backward(n, scales, s3, part, w, t, ti, r1):
    shape = jax.ShapeDtypeStruct
    return pl.pallas_call(
        functools.partial(mix_backward, n, *scales),
        out_shape=(shape(w.shape, F32), shape(s3.shape, BF), shape(part.shape, F32)),
        in_specs=[VMEM] * 6,
        out_specs=(VMEM, VMEM, VMEM),
        scratch_shapes=[
            pltpu.VMEM((2,) + s3.shape, BF),
            pltpu.VMEM(s3.shape, BF),
            pltpu.VMEM((n,) + part.shape, F32),
            pltpu.VMEM((2,) + part.shape, F32),
            pltpu.SemaphoreType.DMA((3, 2, 2, n)),
            pltpu.SemaphoreType.DMA((4,)),
        ],
        compiler_params=pltpu.CompilerParams(
            collective_id=1, has_side_effects=True, vmem_limit_bytes=48 << 20
        ),
        name="mix_backward",
    )(s3, part, w, t, ti, r1)


def plane_tables(rows_y, rows_z):
    phase_y = np_phase(np.arange(rows_y), np_freqs(MY, rows_y), rows_y)
    phase_z = np_phase(np.arange(rows_z), np.arange(MZ), rows_z)
    cy, sy, cz, sz = np.cos(phase_y), np.sin(phase_y), np.cos(phase_z), np.sin(phase_z)
    forward_y = np.concatenate([cy, -sy], axis=1).T
    inverse_y = np.concatenate([cy, -sy], axis=1)
    forward_z = np.stack([np.stack([cz, -sz], axis=1), np.stack([sz, cz], axis=1)], axis=0)
    forward_z = forward_z.transpose(3, 2, 0, 1).reshape(2 * MZ, 2 * rows_z)
    cz, sz = cz.T, sz.T
    inverse_z = np.stack([np.stack([cz, sz], axis=1), np.stack([-sz, cz], axis=1)], axis=0)
    inverse_z = inverse_z.transpose(1, 0, 2, 3).reshape(2 * MZ, 2 * rows_z)
    rows = np.concatenate([forward_y, forward_z, inverse_z], axis=0)
    return [jnp.asarray(v.astype(ml_dtypes.bfloat16)) for v in (rows, inverse_y)]


def table_rows(tables):
    size = tables.shape[0] // 3
    return [tables[k * size : (k + 1) * size] for k in range(3)]


def piece_layout(n):
    count = MY * MZ // n
    wide = max(count // MZ, 1)
    deep = count // wide
    return wide, deep, wide * 16


def pack_planes(acc, kbuf, out):
    planes, n = acc.shape[0], out.shape[0]
    wide, deep, width = piece_layout(n)
    for x in range(planes):
        for g in range(kbuf.shape[0]):
            kbuf[g, pl.ds(x, 2 * MZ, stride=planes), :] = acc[x, :, g * 128 : (g + 1) * 128]
    group = 128 // width
    for j in range(n):
        m0 = j * wide * deep // MZ
        k0 = j * wide * deep % MZ if wide == 1 else 0
        for first in range(0, deep, group):
            parts = [
                kbuf[
                    m0 * 16 // 128,
                    (k0 + first + q) * 2 * planes : (k0 + first + q + 1) * 2 * planes,
                    m0 * 16 % 128 : m0 * 16 % 128 + width,
                ]
                for q in range(group)
            ]
            out[j, :, first * width : first * width + 128] = jnp.concatenate(
                parts, axis=1
            ).astype(BF)


def unpack_planes(received, kbuf, staged):
    planes, n = staged.shape[0], received.shape[0]
    wide, deep, width = piece_layout(n)
    group = 128 // width
    for k in range(MZ):
        owners = [j for j in range(n) if wide > 1 or j % (MZ // deep) == k // deep]
        lane = (k % deep) * width
        low = lane // 128 * 128
        for first in range(0, len(owners), group):
            parts = [
                received[j, :, low : low + 128].astype(F32)[:, lane - low : lane - low + width]
                for j in owners[first : first + group]
            ]
            kbuf[first // group, k * 2 * planes : (k + 1) * 2 * planes, :] = jnp.concatenate(
                parts, axis=1
            )
    for x in range(planes):
        for g in range(kbuf.shape[0]):
            staged[x, :, g * 128 : (g + 1) * 128] = kbuf[
                g, pl.ds(x, 2 * MZ, stride=planes), :
            ].astype(BF)


def plane_forward(source, fy, fz, lines, acc, x):
    channels = source.shape[0]
    rows = 2 * MY
    for c in range(0, channels, 2):
        couple = jnp.concatenate([source[c, 0], source[c + 1, 0]], axis=1)
        result = jnp.dot(fy, couple, preferred_element_type=F32)
        half = result.shape[1] // 2
        lines[pl.ds(c, rows, stride=channels), :] = result[:, :half]
        lines[pl.ds(c + 1, rows, stride=channels), :] = result[:, half:]
    half = MY * channels
    both = jnp.concatenate([lines[:half].astype(BF), lines[half:].astype(BF)], axis=1)
    acc[x] = lax.dot_general(fz, both, (((1,), (1,)), ((), ())), preferred_element_type=F32)


def spread_map(weight, spread, turned):
    size = spread.shape[0]
    place = lax.broadcasted_iota(jnp.int32, (size, weight.shape[0]), 0) >> 4
    lane = lax.broadcasted_iota(jnp.int32, (size, weight.shape[0]), 1)
    copies = jnp.where(place == lane, 1.0, 0.0).astype(BF)
    contracted = 0 if turned else 1
    rows = lax.dot_general(
        copies, weight[...], (((1,), (contracted,)), ((), ())), preferred_element_type=F32
    ).astype(BF)
    full = lax.dot_general(rows, copies, (((1,), (1,)), ((), ())), preferred_element_type=F32)
    row = lax.broadcasted_iota(jnp.int32, (size, size), 0)
    col = lax.broadcasted_iota(jnp.int32, (size, size), 1)
    spread[...] = jnp.where((row & 15) == (col & 15), full, 0.0).astype(BF)


def plane_inverse(staged, iz, iy, factor, lines, pre, x):
    channels = pre.shape[0]
    half = MY * channels
    rolled = factor * lax.dot_general(
        staged[x], iz, (((0,), (0,)), ((), ())), preferred_element_type=F32
    )
    lines[:half] = rolled[:, : rolled.shape[1] // 2]
    lines[half:] = rolled[:, rolled.shape[1] // 2 :]
    for c in range(0, channels, 2):
        pieces = []
        for at in (c, c + 1):
            pieces.append(lines[pl.ds(at, 2 * MY, stride=channels), :].astype(BF))
        result = jnp.dot(
            iy[...], jnp.concatenate(pieces, axis=1), preferred_element_type=F32
        )
        pre[c] = result[:, : result.shape[1] // 2]
        pre[c + 1] = result[:, result.shape[1] // 2 :]


def field_forward(field, tables, out, lines, acc, kbuf):
    x = pl.program_id(0)
    fy, fz, _ = table_rows(tables)
    plane_forward(field, fy, fz, lines, acc, x)

    @pl.when(x == pl.num_programs(0) - 1)
    def _():
        pack_planes(acc, kbuf, out)


def tile_rows(ref, step):
    parts = []
    for half in range(2):
        at = slice((2 * step + half) * 16, (2 * step + half + 1) * 16)
        value = ref[:, 0, at, :]
        parts.append(value.reshape(value.shape[0] * 16, value.shape[2]))
    return jnp.concatenate(parts, axis=1)


GELU_K = math.sqrt(2.0 / math.pi)
GELU_C = 0.044715


def gelu_slope(value):
    square = value * value
    bent = jnp.tanh(value * (GELU_K + (GELU_K * GELU_C) * square))
    side = value * (0.5 * GELU_K + (1.5 * GELU_K * GELU_C) * square)
    return (1.0 + bent) * (0.5 + (1.0 - bent) * side)


def middle(
    factor, received, field, cot, weight, bias, tables, iy,
    dpre, out, part, lines, acc, kbuf, staged, pre, spread, outer, sums, shift,
):
    x = pl.program_id(0)
    fy, fz, iz = table_rows(tables)
    channels = field.shape[0]

    @pl.when(x == 0)
    def _():
        unpack_planes(received, kbuf, staged)
        spread_map(weight, spread, False)
        row = lax.broadcasted_iota(jnp.int32, (channels, channels), 0)
        col = lax.broadcasted_iota(jnp.int32, (channels, channels), 1)
        column = jnp.sum(jnp.where(row == col, bias[...], 0.0), axis=1, keepdims=True)
        shift[...] = jnp.broadcast_to(column, shift.shape)
        outer[...] = jnp.zeros_like(outer)
        sums[...] = jnp.zeros_like(sums)

    plane_inverse(staged, iz, iy, factor, lines, pre, x)

    for at in range(field.shape[2] // 32):
        tile = tile_rows(field, at)
        mixed = jnp.dot(spread[...], tile, preferred_element_type=F32)
        width = mixed.shape[1] // 2
        halves = []
        for half in range(2):
            rows = slice((2 * at + half) * 16, (2 * at + half + 1) * 16)
            value = mixed[:, half * width : (half + 1) * width].reshape(channels, 16, width)
            value = value + pre[:, rows, :] + shift[...][:, None, :]
            slope = gelu_slope(value) * cot[:, 0, rows, :].astype(F32)
            rounded = slope.astype(BF)
            dpre[:, 0, rows, :] = rounded
            wide = rounded.astype(F32)
            sums[...] += wide[:, :8] + wide[:, 8:]
            halves.append(rounded.reshape(channels * 16, width))
        outer[...] += lax.dot_general(
            tile, jnp.concatenate(halves, axis=1), (((1,), (1,)), ((), ())),
            preferred_element_type=F32,
        )
    plane_forward(dpre, fy, fz, lines, acc, x)

    @pl.when(x == pl.num_programs(0) - 1)
    def _():
        pack_planes(acc, kbuf, out)
        size = channels * 16
        row = lax.broadcasted_iota(jnp.int32, (size, size), 0)
        col = lax.broadcasted_iota(jnp.int32, (size, size), 1)
        kept = jnp.where((row & 15) == (col & 15), outer[...], 0.0)
        kept = jnp.sum(kept.reshape(channels, 16, size), axis=1)
        place = lax.broadcasted_iota(jnp.int32, (size, 128), 0) >> 4
        lane = lax.broadcasted_iota(jnp.int32, (size, 128), 1)
        gather = jnp.where(place == lane, 1.0, 0.0).astype(F32)
        part[:channels] = jnp.dot(
            kept, gather, preferred_element_type=F32, precision=lax.Precision.HIGHEST
        )
        part[channels:] = jnp.sum(sums[...], axis=1)


def last(factor, received, dpre, weight, tables, iy, grad, lines, kbuf, staged, pre, spread):
    x = pl.program_id(0)
    iz = table_rows(tables)[2]
    channels = dpre.shape[0]

    @pl.when(x == 0)
    def _():
        unpack_planes(received, kbuf, staged)
        spread_map(weight, spread, True)

    plane_inverse(staged, iz, iy, factor, lines, pre, x)

    for at in range(dpre.shape[2] // 32):
        mixed = jnp.dot(spread[...], tile_rows(dpre, at), preferred_element_type=F32)
        width = mixed.shape[1] // 2
        for half in range(2):
            rows = slice((2 * at + half) * 16, (2 * at + half + 1) * 16)
            value = mixed[:, half * width : (half + 1) * width].reshape(channels, 16, width)
            grad[:, 0, rows, :] = (value + pre[:, rows, :]).astype(BF)


def whole(array):
    zeros = (0,) * array.ndim
    return pl.BlockSpec(array.shape, lambda x: zeros)


def plane_block(array):
    c, _, y, z = array.shape
    return pl.BlockSpec((c, 1, y, z), lambda x: (0, x, 0, 0))


def scratch(field, *names):
    c, planes, y, z = field.shape
    every = {
        "lines": pltpu.VMEM((2 * MY * c, z), F32),
        "acc": pltpu.VMEM((planes, 2 * MZ, MY * c), F32),
        "kbuf": pltpu.VMEM((MY * c // 128, 2 * MZ * planes, 128), F32),
        "staged": pltpu.VMEM((planes, 2 * MZ, MY * c), BF),
        "pre": pltpu.VMEM((c, y, z), F32),
        "spread": pltpu.VMEM((16 * c, 16 * c), BF),
        "outer": pltpu.VMEM((16 * c, 16 * c), F32),
        "shift": pltpu.VMEM((c, z), F32),
        "sums": pltpu.VMEM((c, 8, z), F32),
    }
    return [every[name] for name in names]


def params():
    return pltpu.CompilerParams(vmem_limit_bytes=48 << 20)


def run_first(n, field, tables):
    c, planes, _, _ = field.shape
    out = jax.ShapeDtypeStruct((n, 2 * planes, MY * MZ // n * c), BF)
    return pl.pallas_call(
        field_forward,
        grid=(planes,),
        out_shape=out,
        in_specs=[plane_block(field), whole(tables)],
        out_specs=whole(out),
        scratch_shapes=scratch(field, "lines", "acc", "kbuf"),
        compiler_params=params(),
        name="field_forward",
    )(field, tables)


def run_middle(factor, received, field, cot, weight, bias, tables, iy):
    c, planes, _, _ = field.shape
    out = jax.ShapeDtypeStruct(received.shape, BF)
    part = jax.ShapeDtypeStruct((2 * c, 128), F32)
    flat = [weight, bias, tables, iy]
    return pl.pallas_call(
        functools.partial(middle, factor),
        grid=(planes,),
        out_shape=(jax.ShapeDtypeStruct(field.shape, BF), out, part),
        in_specs=[whole(received), plane_block(field), plane_block(cot)] + [whole(v) for v in flat],
        out_specs=(plane_block(field), whole(out), whole(part)),
        scratch_shapes=scratch(
            field, "lines", "acc", "kbuf", "staged", "pre", "spread", "outer", "sums", "shift"
        ),
        compiler_params=params(),
        name="middle",
    )(received, field, cot, *flat)


def run_last(factor, received, dpre, weight, tables, iy):
    c, planes, _, _ = dpre.shape
    flat = [weight, tables, iy]
    return pl.pallas_call(
        functools.partial(last, factor),
        grid=(planes,),
        out_shape=jax.ShapeDtypeStruct(dpre.shape, BF),
        in_specs=[whole(received), plane_block(dpre)] + [whole(v) for v in flat],
        out_specs=plane_block(dpre),
        scratch_shapes=scratch(dpre, "lines", "kbuf", "staged", "pre", "spread"),
        compiler_params=params(),
        name="last",
    )(received, dpre, *flat)


def body(field, cotangent, spectral_weight, point_weight, point_bias):
    samples, channels, planes, rows_y, rows_z = field.shape
    n = lax.axis_size("slab")
    total_samples = samples * lax.axis_size("batch")
    cells = n * planes * rows_y * rows_z
    scale_f = 1.0 / math.sqrt(cells)
    scale_i = 1.0 / math.sqrt(MX * MY * MZ)
    scale_p = 1.0 / math.sqrt(total_samples * cells)
    scale_w = math.sqrt(MX * MY * MZ / (total_samples * cells))
    tables, iy = plane_tables(rows_y, rows_z)
    t, ti = x_tables(n, planes)
    f = field.reshape(field.shape[1:])
    cot = cotangent.reshape(cotangent.shape[1:])
    s1 = run_first(n, f, tables)
    r1, r2 = run_forward(n, scale_f, s1, spectral_weight, t, ti)
    bias = point_bias[None, :]
    dpre, s3, part = run_middle(
        scale_i, r2, f, cot, point_weight, bias, tables, iy
    )
    grad_spec, r4, total = run_backward(
        n, (scale_f, scale_i, scale_w), s3, part, spectral_weight, t, ti, r1
    )
    input_grad = run_last(scale_f, r4, dpre, point_weight, tables, iy)
    return (
        input_grad[None],
        grad_spec,
        scale_p * total[:channels, :channels],
        scale_p * jnp.sum(total[channels:], axis=1),
    )


def solution(mesh):
    placed = (
        P("batch", None, "slab", None, None),
        P("batch", None, "slab", None, None),
        P("slab", None, None, None),
        P(),
        P(),
    )
    return jax.shard_map(
        body,
        mesh=mesh,
        in_specs=placed,
        out_specs=(P("batch", None, "slab", None, None), P("slab", None, None, None), P(), P()),
        check_vma=False,
    )
```

```python
import functools
import math

import jax
import jax.numpy as jnp
import ml_dtypes
import numpy as np
from jax import lax
from jax.experimental import pallas as pl
from jax.experimental.pallas import tpu as pltpu
from jax.sharding import PartitionSpec as P

MX = 32
MY = 32
MZ = 32
PB = 16
BF = jnp.bfloat16
F32 = jnp.float32
MESH = pl.DeviceIdType.MESH
VMEM = pl.BlockSpec(memory_space=pltpu.VMEM)


def np_freqs(number, length):
    indices = np.arange(number)
    return np.where(indices < number // 2, indices, indices + (length - number))


def np_phase(positions, frequencies, length):
    product = positions[:, None] * frequencies[None, :] % length
    return product.astype(np.float64) * (2.0 * math.pi / length)


def x_tables(n, planes):
    total = n * planes
    phase = np_phase(np.arange(total), np_freqs(MX, total), total)
    cosine, sine = np.cos(phase), np.sin(phase)
    forward = np.stack(
        [np.stack([cosine, -sine], axis=1), np.stack([sine, cosine], axis=1)], axis=0
    )
    inverse = np.stack(
        [np.stack([cosine, -sine], axis=1), np.stack([sine, cosine], axis=1)], axis=0
    )

    def rows(table, copies):
        table = table.reshape(2, n, planes, 2, MX).transpose(1, 0, 2, 3, 4)
        table = table.reshape(n * 2 * planes, 2, 1, MX)
        table = np.broadcast_to(table, (table.shape[0], 2, copies, MX))
        return table.reshape(table.shape[0], 2 * copies * MX).astype(ml_dtypes.bfloat16)

    return jnp.asarray(rows(forward, 4)), jnp.asarray(rows(inverse, 4))


def enter(n, me, bat):
    barrier = pltpu.get_barrier_semaphore()

    def greet(k, carry):
        pl.semaphore_signal(
            barrier, inc=1, device_id={"slab": lax.rem(me + k, n)}, device_id_type=MESH
        )
        return carry

    lax.fori_loop(1, n, greet, 0)
    pl.semaphore_signal(barrier, inc=1, device_id={"batch": 1 - bat}, device_id_type=MESH)
    pl.semaphore_wait(barrier, n)


def peer_copy(n, me, k, source, target, landed, sems):
    to = lax.rem(me + k, n)
    return pltpu.make_async_remote_copy(
        src_ref=source(to),
        dst_ref=target(landed),
        send_sem=sems.at[0, k],
        recv_sem=sems.at[1, k],
        device_id={"slab": to},
        device_id_type=MESH,
    )


def send_all(n, me, source, target, sems):
    def step(i, carry):
        k = n // 2 + (i + 1) // 2 * (2 * (i % 2) - 1)
        peer_copy(n, me, k, source, target, me, sems).start()
        return carry

    lax.fori_loop(0, n - 1, step, 0)


def wait_landed(n, me, source, target, sems):
    def step(k, carry):
        peer_copy(n, me, k, source, target, lax.rem(me - k + n, n), sems).wait_recv()
        return carry

    lax.fori_loop(1, n, step, 0)


def wait_sent(n, me, source, target, sems):
    def step(k, carry):
        peer_copy(n, me, k, source, target, me, sems).wait_send()
        return carry

    lax.fori_loop(1, n, step, 0)


def part_count(lanes):
    return min(4, lanes // 128)


def in_parts(source, target, sems):
    parts = part_count(source.shape[2])
    lanes = source.shape[2] // parts
    return [
        (
            lambda to, at=pl.ds(h * lanes, lanes): source.at[to, :, at],
            lambda slot, at=pl.ds(h * lanes, lanes): target.at[slot, :, at],
            sems.at[h],
        )
        for h in range(parts)
    ]


def block_pairs(count):
    return min(PB, count // part_count(count * 16))


def block_lanes(block, pairs):
    return pl.ds(pl.multiple_of(block * (pairs * 16), 128), pairs * 16)


def four(values):
    return jnp.concatenate([values] * 4, axis=-1)


def expand(planes_ref, slot, block, pairs, table_ref):
    rows = planes_ref.shape[1] * planes_ref.shape[2]
    part = planes_ref[slot, :, :, block_lanes(block, pairs)].reshape(rows, pairs * 16)
    both = lax.dot_general(
        part, table_ref[...], (((0,), (0,)), ((), ())), preferred_element_type=F32
    )
    half = both.shape[1] // 2
    return (
        both[:, :half].reshape(pairs, 16, half),
        both[:, half:].reshape(pairs, 16, half),
    )


def own_mask(channels):
    shape = (channels, channels * MX)
    row = lax.broadcasted_iota(jnp.int32, shape, 0)
    col = lax.broadcasted_iota(jnp.int32, shape, 1)
    low = row * MX
    return jnp.where((col >= low) & (col < low + MX), 1.0, 0.0).astype(F32)


def lane_fold(values):
    quarter = values.shape[-1] // 4
    return (
        values[..., :quarter]
        + values[..., quarter : 2 * quarter]
        + values[..., 2 * quarter : 3 * quarter]
        + values[..., 3 * quarter :]
    )


def contract(first, second, table_ref, out_ref, block, pairs):
    both = jnp.concatenate([lane_fold(first), lane_fold(second)], axis=-1)
    both = both.reshape(pairs * 16, both.shape[-1]).astype(BF)
    result = lax.dot_general(
        table_ref[...], both, (((1,), (1,)), ((), ())), preferred_element_type=F32
    )
    out_ref[:, :, block_lanes(block, pairs)] = result.astype(BF).reshape(
        out_ref.shape[0], out_ref.shape[1], pairs * 16
    )


def pair_places(count, block, pairs):
    wide = max(count // MZ, 1)
    deep = count // wide
    step = pairs // wide
    return [m * deep + block * step + k for k in range(step) for m in range(wide)]


def weight_pair(w_ref, block, pairs):
    places = pair_places(w_ref.shape[0], block, pairs)
    return tuple(
        jnp.stack([w_ref[at, part].astype(F32) for at in places], axis=0) for part in range(2)
    )


def mix_forward(n, scale, s1, w, t, ti, r1, r2, s2, sems, pair):
    me = lax.axis_index("slab")
    bat = lax.axis_index("batch")
    enter(n, me, bat)
    one = in_parts(s1, r1.at[bat], sems.at[0])
    two = in_parts(s2, r2, sems.at[1])
    pairs = block_pairs(w.shape[0])
    blocks = w.shape[0] // pairs // len(one)
    for each in one:
        send_all(n, me, *each)
    r1[bat, me] = s1[me]
    cross = pltpu.make_async_remote_copy(
        src_ref=r1.at[bat],
        dst_ref=r1.at[bat],
        send_sem=pair.at[0],
        recv_sem=pair.at[1],
        device_id={"batch": 1 - bat},
        device_id_type=MESH,
    )
    mask = own_mask(16)[None]

    def step(block, carry):
        u0, u1 = expand(r1, bat, block, pairs, t)
        u0, u1 = four(u0 * scale), four(u1 * scale)
        w0, w1 = weight_pair(w, block, pairs)
        v0 = jnp.sum(u0 * w0 - u1 * w1, axis=1, keepdims=True) * mask
        v1 = jnp.sum(u0 * w1 + u1 * w0, axis=1, keepdims=True) * mask
        contract(v0, v1, ti, s2, block, pairs)
        return carry

    for h in range(len(one)):
        wait_landed(n, me, *one[h])
        if h == len(one) - 1:
            cross.start()
        lax.fori_loop(h * blocks, (h + 1) * blocks, step, 0)
        send_all(n, me, *two[h])
    r2[me] = s2[me]
    cross.wait()
    for each in one:
        wait_sent(n, me, *each)
    for each in two:
        wait_landed(n, me, *each)
        wait_sent(n, me, *each)


def mix_backward(
    n, scale_f, scale_i, scale_w, s3, part, w, t, ti, r1, grad, r4, total,
    r3, s4, slots, half, sems, pair,
):
    me = lax.axis_index("slab")
    bat = lax.axis_index("batch")
    enter(n, me, bat)
    one = in_parts(s3, r3.at[bat], sems.at[0])
    two = in_parts(s4, r4, sems.at[1])
    small = (lambda to: part, lambda at: slots.at[at], sems.at[2, 0])
    pairs = block_pairs(w.shape[0])
    blocks = w.shape[0] // pairs // len(one)
    for each in one:
        send_all(n, me, *each)
    send_all(n, me, *small)
    r3[bat, me] = s3[me]
    slots[me] = part[...]

    def across(source, target, at):
        return pltpu.make_async_remote_copy(
            src_ref=source,
            dst_ref=target,
            send_sem=pair.at[2 * at],
            recv_sem=pair.at[2 * at + 1],
            device_id={"batch": 1 - bat},
            device_id_type=MESH,
        )

    cross = across(r3.at[bat], r3.at[bat], 0)
    mask = own_mask(16)[None]

    def gradient(slot, block):
        d0, d1 = expand(r3, slot, block, pairs, t)
        d0, d1 = four(d0), four(d1)
        d0 = jnp.sum(d0 * mask, axis=1, keepdims=True) * scale_i
        d1 = jnp.sum(d1 * mask, axis=1, keepdims=True) * scale_i
        return d0, d1

    def step(block, carry):
        d0, d1 = gradient(bat, block)
        w0, w1 = weight_pair(w, block, pairs)
        contract(d0 * w0 + d1 * w1, d1 * w0 - d0 * w1, ti, s4, block, pairs)
        return carry

    for h in range(len(one)):
        wait_landed(n, me, *one[h])
        if h == len(one) - 1:
            cross.start()
        lax.fori_loop(h * blocks, (h + 1) * blocks, step, 0)
        send_all(n, me, *two[h])
    r4[me] = s4[me]
    wait_landed(n, me, *small)
    wait_sent(n, me, *small)
    summed = slots[0]
    for at in range(1, n):
        summed = summed + slots[at]
    half[bat] = summed
    other = across(half.at[bat], half.at[bat], 1)
    other.start()
    cross.wait()

    def outer(block, carry):
        places = pair_places(w.shape[0], block, pairs)
        first = None
        for slot in range(2):
            u0, u1 = expand(r1, slot, block, pairs, t)
            u0, u1 = four(u0), four(u1)
            d0, d1 = gradient(slot, block)
            d0, d1 = d0 * (scale_f * scale_w), d1 * (scale_f * scale_w)
            real = u0 * d0 + u1 * d1
            imag = u0 * d1 - u1 * d0
            if first is None:
                first = (real, imag)
            else:
                real, imag = first[0] + real, first[1] + imag
                for row, at in enumerate(places):
                    grad[at, 0] = real[row]
                    grad[at, 1] = imag[row]
        return carry

    lax.fori_loop(0, len(one) * blocks, outer, 0)
    other.wait()
    total[...] = half[0] + half[1]
    for each in one:
        wait_sent(n, me, *each)
    for each in two:
        wait_landed(n, me, *each)
        wait_sent(n, me, *each)


def run_forward(n, scale, s1, w, t, ti):
    shape = jax.ShapeDtypeStruct
    return pl.pallas_call(
        functools.partial(mix_forward, n, scale),
        out_shape=(shape((2,) + s1.shape, BF), shape(s1.shape, BF)),
        in_specs=[VMEM] * 4,
        out_specs=(VMEM, VMEM),
        scratch_shapes=[
            pltpu.VMEM(s1.shape, BF),
            pltpu.SemaphoreType.DMA((2, 4, 2, n)),
            pltpu.SemaphoreType.DMA((2,)),
        ],
        compiler_params=pltpu.CompilerParams(
            collective_id=0, has_side_effects=True, vmem_limit_bytes=40 << 20
        ),
        name="mix_forward",
    )(s1, w, t, ti)


def run_backward(n, scales, s3, part, w, t, ti, r1):
    shape = jax.ShapeDtypeStruct
    return pl.pallas_call(
        functools.partial(mix_backward, n, *scales),
        out_shape=(shape(w.shape, F32), shape(s3.shape, BF), shape(part.shape, F32)),
        in_specs=[VMEM] * 6,
        out_specs=(VMEM, VMEM, VMEM),
        scratch_shapes=[
            pltpu.VMEM((2,) + s3.shape, BF),
            pltpu.VMEM(s3.shape, BF),
            pltpu.VMEM((n,) + part.shape, F32),
            pltpu.VMEM((2,) + part.shape, F32),
            pltpu.SemaphoreType.DMA((3, 4, 2, n)),
            pltpu.SemaphoreType.DMA((4,)),
        ],
        compiler_params=pltpu.CompilerParams(
            collective_id=1, has_side_effects=True, vmem_limit_bytes=48 << 20
        ),
        name="mix_backward",
    )(s3, part, w, t, ti, r1)


def plane_tables(rows_y, rows_z):
    phase_y = np_phase(np.arange(rows_y), np_freqs(MY, rows_y), rows_y)
    phase_z = np_phase(np.arange(rows_z), np.arange(MZ), rows_z)
    cy, sy, cz, sz = np.cos(phase_y), np.sin(phase_y), np.cos(phase_z), np.sin(phase_z)
    forward_y = np.concatenate([cy, -sy], axis=1).T
    inverse_y = np.concatenate([cy, -sy], axis=1)
    forward_z = np.stack([np.stack([cz, -sz], axis=1), np.stack([sz, cz], axis=1)], axis=0)
    forward_z = forward_z.transpose(3, 2, 0, 1).reshape(2 * MZ, 2 * rows_z)
    cz, sz = cz.T, sz.T
    inverse_z = np.stack([np.stack([cz, sz], axis=1), np.stack([-sz, cz], axis=1)], axis=0)
    inverse_z = inverse_z.transpose(1, 0, 2, 3).reshape(2 * MZ, 2 * rows_z)
    rows = np.concatenate([forward_y, forward_z, inverse_z], axis=0)
    return [jnp.asarray(v.astype(ml_dtypes.bfloat16)) for v in (rows, inverse_y)]


def table_rows(tables):
    size = tables.shape[0] // 3
    return [tables[k * size : (k + 1) * size] for k in range(3)]


def piece_layout(n):
    count = MY * MZ // n
    wide = max(count // MZ, 1)
    deep = count // wide
    return wide, deep, wide * 16


def pack_planes(acc, kbuf, out):
    planes, n = acc.shape[0], out.shape[0]
    wide, deep, width = piece_layout(n)
    for x in range(planes):
        for g in range(kbuf.shape[0]):
            kbuf[g, pl.ds(x, 2 * MZ, stride=planes), :] = acc[x, :, g * 128 : (g + 1) * 128]
    group = 128 // width
    for j in range(n):
        m0 = j * wide * deep // MZ
        k0 = j * wide * deep % MZ if wide == 1 else 0
        for first in range(0, deep, group):
            parts = [
                kbuf[
                    m0 * 16 // 128,
                    (k0 + first + q) * 2 * planes : (k0 + first + q + 1) * 2 * planes,
                    m0 * 16 % 128 : m0 * 16 % 128 + width,
                ]
                for q in range(group)
            ]
            out[j, :, first * width : first * width + 128] = jnp.concatenate(
                parts, axis=1
            ).astype(BF)


def unpack_planes(received, kbuf, staged):
    planes, n = staged.shape[0], received.shape[0]
    wide, deep, width = piece_layout(n)
    group = 128 // width
    for k in range(MZ):
        owners = [j for j in range(n) if wide > 1 or j % (MZ // deep) == k // deep]
        lane = (k % deep) * width
        low = lane // 128 * 128
        for first in range(0, len(owners), group):
            parts = [
                received[j, :, low : low + 128].astype(F32)[:, lane - low : lane - low + width]
                for j in owners[first : first + group]
            ]
            kbuf[first // group, k * 2 * planes : (k + 1) * 2 * planes, :] = jnp.concatenate(
                parts, axis=1
            )
    for x in range(planes):
        for g in range(kbuf.shape[0]):
            staged[x, :, g * 128 : (g + 1) * 128] = kbuf[
                g, pl.ds(x, 2 * MZ, stride=planes), :
            ].astype(BF)


def plane_forward(source, fy, fz, lines, acc, x):
    channels = source.shape[0]
    rows = 2 * MY
    for c in range(0, channels, 2):
        couple = jnp.concatenate([source[c, 0], source[c + 1, 0]], axis=1)
        result = jnp.dot(fy, couple, preferred_element_type=F32)
        half = result.shape[1] // 2
        lines[pl.ds(c, rows, stride=channels), :] = result[:, :half]
        lines[pl.ds(c + 1, rows, stride=channels), :] = result[:, half:]
    half = MY * channels
    both = jnp.concatenate([lines[:half].astype(BF), lines[half:].astype(BF)], axis=1)
    acc[x] = lax.dot_general(fz, both, (((1,), (1,)), ((), ())), preferred_element_type=F32)


def spread_map(weight, spread, turned):
    size = spread.shape[0]
    place = lax.broadcasted_iota(jnp.int32, (size, weight.shape[0]), 0) >> 4
    lane = lax.broadcasted_iota(jnp.int32, (size, weight.shape[0]), 1)
    copies = jnp.where(place == lane, 1.0, 0.0).astype(BF)
    contracted = 0 if turned else 1
    rows = lax.dot_general(
        copies, weight[...], (((1,), (contracted,)), ((), ())), preferred_element_type=F32
    ).astype(BF)
    full = lax.dot_general(rows, copies, (((1,), (1,)), ((), ())), preferred_element_type=F32)
    row = lax.broadcasted_iota(jnp.int32, (size, size), 0)
    col = lax.broadcasted_iota(jnp.int32, (size, size), 1)
    spread[...] = jnp.where((row & 15) == (col & 15), full, 0.0).astype(BF)


def plane_inverse(staged, iz, iy, factor, lines, pre, x):
    channels = pre.shape[0]
    half = MY * channels
    rolled = factor * lax.dot_general(
        staged[x], iz, (((0,), (0,)), ((), ())), preferred_element_type=F32
    )
    lines[:half] = rolled[:, : rolled.shape[1] // 2]
    lines[half:] = rolled[:, rolled.shape[1] // 2 :]
    for c in range(0, channels, 2):
        pieces = []
        for at in (c, c + 1):
            pieces.append(lines[pl.ds(at, 2 * MY, stride=channels), :].astype(BF))
        result = jnp.dot(
            iy[...], jnp.concatenate(pieces, axis=1), preferred_element_type=F32
        )
        pre[c] = result[:, : result.shape[1] // 2]
        pre[c + 1] = result[:, result.shape[1] // 2 :]


def field_forward(field, tables, out, lines, acc, kbuf):
    x = pl.program_id(0)
    fy, fz, _ = table_rows(tables)
    plane_forward(field, fy, fz, lines, acc, x)

    @pl.when(x == pl.num_programs(0) - 1)
    def _():
        pack_planes(acc, kbuf, out)


def tile_rows(ref, step):
    parts = []
    for half in range(2):
        at = slice((2 * step + half) * 16, (2 * step + half + 1) * 16)
        value = ref[:, 0, at, :]
        parts.append(value.reshape(value.shape[0] * 16, value.shape[2]))
    return jnp.concatenate(parts, axis=1)


GELU_K = math.sqrt(2.0 / math.pi)
GELU_C = 0.044715


def gelu_slope(value):
    square = value * value
    bent = jnp.tanh(value * (GELU_K + (GELU_K * GELU_C) * square))
    side = value * (0.5 * GELU_K + (1.5 * GELU_K * GELU_C) * square)
    return (1.0 + bent) * (0.5 + (1.0 - bent) * side)


def middle(
    factor, received, field, cot, weight, bias, tables, iy,
    dpre, out, part, lines, acc, kbuf, staged, pre, spread, outer, sums, shift,
):
    x = pl.program_id(0)
    fy, fz, iz = table_rows(tables)
    channels = field.shape[0]

    @pl.when(x == 0)
    def _():
        unpack_planes(received, kbuf, staged)
        spread_map(weight, spread, False)
        row = lax.broadcasted_iota(jnp.int32, (channels, channels), 0)
        col = lax.broadcasted_iota(jnp.int32, (channels, channels), 1)
        column = jnp.sum(jnp.where(row == col, bias[...], 0.0), axis=1, keepdims=True)
        shift[...] = jnp.broadcast_to(column, shift.shape)
        outer[...] = jnp.zeros_like(outer)
        sums[...] = jnp.zeros_like(sums)

    plane_inverse(staged, iz, iy, factor, lines, pre, x)

    for at in range(field.shape[2] // 32):
        tile = tile_rows(field, at)
        mixed = jnp.dot(spread[...], tile, preferred_element_type=F32)
        width = mixed.shape[1] // 2
        halves = []
        for half in range(2):
            rows = slice((2 * at + half) * 16, (2 * at + half + 1) * 16)
            value = mixed[:, half * width : (half + 1) * width].reshape(channels, 16, width)
            value = value + pre[:, rows, :] + shift[...][:, None, :]
            slope = gelu_slope(value) * cot[:, 0, rows, :].astype(F32)
            rounded = slope.astype(BF)
            dpre[:, 0, rows, :] = rounded
            wide = rounded.astype(F32)
            sums[...] += wide[:, :8] + wide[:, 8:]
            halves.append(rounded.reshape(channels * 16, width))
        outer[...] += lax.dot_general(
            tile, jnp.concatenate(halves, axis=1), (((1,), (1,)), ((), ())),
            preferred_element_type=F32,
        )
    plane_forward(dpre, fy, fz, lines, acc, x)

    @pl.when(x == pl.num_programs(0) - 1)
    def _():
        pack_planes(acc, kbuf, out)
        size = channels * 16
        row = lax.broadcasted_iota(jnp.int32, (size, size), 0)
        col = lax.broadcasted_iota(jnp.int32, (size, size), 1)
        kept = jnp.where((row & 15) == (col & 15), outer[...], 0.0)
        kept = jnp.sum(kept.reshape(channels, 16, size), axis=1)
        place = lax.broadcasted_iota(jnp.int32, (size, 128), 0) >> 4
        lane = lax.broadcasted_iota(jnp.int32, (size, 128), 1)
        gather = jnp.where(place == lane, 1.0, 0.0).astype(F32)
        part[:channels] = jnp.dot(
            kept, gather, preferred_element_type=F32, precision=lax.Precision.HIGHEST
        )
        part[channels:] = jnp.sum(sums[...], axis=1)


def last(factor, received, dpre, weight, tables, iy, grad, lines, kbuf, staged, pre, spread):
    x = pl.program_id(0)
    iz = table_rows(tables)[2]
    channels = dpre.shape[0]

    @pl.when(x == 0)
    def _():
        unpack_planes(received, kbuf, staged)
        spread_map(weight, spread, True)

    plane_inverse(staged, iz, iy, factor, lines, pre, x)

    for at in range(dpre.shape[2] // 32):
        mixed = jnp.dot(spread[...], tile_rows(dpre, at), preferred_element_type=F32)
        width = mixed.shape[1] // 2
        for half in range(2):
            rows = slice((2 * at + half) * 16, (2 * at + half + 1) * 16)
            value = mixed[:, half * width : (half + 1) * width].reshape(channels, 16, width)
            grad[:, 0, rows, :] = (value + pre[:, rows, :]).astype(BF)


def whole(array):
    zeros = (0,) * array.ndim
    return pl.BlockSpec(array.shape, lambda x: zeros)


def plane_block(array):
    c, _, y, z = array.shape
    return pl.BlockSpec((c, 1, y, z), lambda x: (0, x, 0, 0))


def scratch(field, *names):
    c, planes, y, z = field.shape
    every = {
        "lines": pltpu.VMEM((2 * MY * c, z), F32),
        "acc": pltpu.VMEM((planes, 2 * MZ, MY * c), F32),
        "kbuf": pltpu.VMEM((MY * c // 128, 2 * MZ * planes, 128), F32),
        "staged": pltpu.VMEM((planes, 2 * MZ, MY * c), BF),
        "pre": pltpu.VMEM((c, y, z), F32),
        "spread": pltpu.VMEM((16 * c, 16 * c), BF),
        "outer": pltpu.VMEM((16 * c, 16 * c), F32),
        "shift": pltpu.VMEM((c, z), F32),
        "sums": pltpu.VMEM((c, 8, z), F32),
    }
    return [every[name] for name in names]


def params():
    return pltpu.CompilerParams(vmem_limit_bytes=48 << 20)


def run_first(n, field, tables):
    c, planes, _, _ = field.shape
    out = jax.ShapeDtypeStruct((n, 2 * planes, MY * MZ // n * c), BF)
    return pl.pallas_call(
        field_forward,
        grid=(planes,),
        out_shape=out,
        in_specs=[plane_block(field), whole(tables)],
        out_specs=whole(out),
        scratch_shapes=scratch(field, "lines", "acc", "kbuf"),
        compiler_params=params(),
        name="field_forward",
    )(field, tables)


def run_middle(factor, received, field, cot, weight, bias, tables, iy):
    c, planes, _, _ = field.shape
    out = jax.ShapeDtypeStruct(received.shape, BF)
    part = jax.ShapeDtypeStruct((2 * c, 128), F32)
    flat = [weight, bias, tables, iy]
    return pl.pallas_call(
        functools.partial(middle, factor),
        grid=(planes,),
        out_shape=(jax.ShapeDtypeStruct(field.shape, BF), out, part),
        in_specs=[whole(received), plane_block(field), plane_block(cot)] + [whole(v) for v in flat],
        out_specs=(plane_block(field), whole(out), whole(part)),
        scratch_shapes=scratch(
            field, "lines", "acc", "kbuf", "staged", "pre", "spread", "outer", "sums", "shift"
        ),
        compiler_params=params(),
        name="middle",
    )(received, field, cot, *flat)


def run_last(factor, received, dpre, weight, tables, iy):
    c, planes, _, _ = dpre.shape
    flat = [weight, tables, iy]
    return pl.pallas_call(
        functools.partial(last, factor),
        grid=(planes,),
        out_shape=jax.ShapeDtypeStruct(dpre.shape, BF),
        in_specs=[whole(received), plane_block(dpre)] + [whole(v) for v in flat],
        out_specs=plane_block(dpre),
        scratch_shapes=scratch(dpre, "lines", "kbuf", "staged", "pre", "spread"),
        compiler_params=params(),
        name="last",
    )(received, dpre, *flat)


def body(field, cotangent, spectral_weight, point_weight, point_bias):
    samples, channels, planes, rows_y, rows_z = field.shape
    n = lax.axis_size("slab")
    total_samples = samples * lax.axis_size("batch")
    cells = n * planes * rows_y * rows_z
    scale_f = 1.0 / math.sqrt(cells)
    scale_i = 1.0 / math.sqrt(MX * MY * MZ)
    scale_p = 1.0 / math.sqrt(total_samples * cells)
    scale_w = math.sqrt(MX * MY * MZ / (total_samples * cells))
    tables, iy = plane_tables(rows_y, rows_z)
    t, ti = x_tables(n, planes)
    f = field.reshape(field.shape[1:])
    cot = cotangent.reshape(cotangent.shape[1:])
    s1 = run_first(n, f, tables)
    r1, r2 = run_forward(n, scale_f, s1, spectral_weight, t, ti)
    bias = point_bias[None, :]
    dpre, s3, part = run_middle(
        scale_i, r2, f, cot, point_weight, bias, tables, iy
    )
    grad_spec, r4, total = run_backward(
        n, (scale_f, scale_i, scale_w), s3, part, spectral_weight, t, ti, r1
    )
    input_grad = run_last(scale_f, r4, dpre, point_weight, tables, iy)
    return (
        input_grad[None],
        grad_spec,
        scale_p * total[:channels, :channels],
        scale_p * jnp.sum(total[channels:], axis=1),
    )


def solution(mesh):
    placed = (
        P("batch", None, "slab", None, None),
        P("batch", None, "slab", None, None),
        P("slab", None, None, None),
        P(),
        P(),
    )
    return jax.shard_map(
        body,
        mesh=mesh,
        in_specs=placed,
        out_specs=(P("batch", None, "slab", None, None), P("slab", None, None, None), P(), P()),
        check_vma=False,
    )
```

```python
import functools
import math

import jax
import jax.numpy as jnp
import ml_dtypes
import numpy as np
from jax import lax
from jax.experimental import pallas as pl
from jax.experimental.pallas import tpu as pltpu
from jax.sharding import PartitionSpec as P

MX = 32
MY = 32
MZ = 32
PB = 16
BF = jnp.bfloat16
F32 = jnp.float32
MESH = pl.DeviceIdType.MESH
VMEM = pl.BlockSpec(memory_space=pltpu.VMEM)


def np_freqs(number, length):
    indices = np.arange(number)
    return np.where(indices < number // 2, indices, indices + (length - number))


def np_phase(positions, frequencies, length):
    product = positions[:, None] * frequencies[None, :] % length
    return product.astype(np.float64) * (2.0 * math.pi / length)


def x_tables(n, planes):
    total = n * planes
    phase = np_phase(np.arange(total), np_freqs(MX, total), total)
    cosine, sine = np.cos(phase), np.sin(phase)
    forward = np.stack(
        [np.stack([cosine, -sine], axis=1), np.stack([sine, cosine], axis=1)], axis=0
    )
    inverse = np.stack(
        [np.stack([cosine, -sine], axis=1), np.stack([sine, cosine], axis=1)], axis=0
    )

    def rows(table, copies):
        table = table.reshape(2, n, planes, 2, MX).transpose(1, 0, 2, 3, 4)
        table = table.reshape(n * 2 * planes, 2, 1, MX)
        table = np.broadcast_to(table, (table.shape[0], 2, copies, MX))
        return table.reshape(table.shape[0], 2 * copies * MX).astype(ml_dtypes.bfloat16)

    return jnp.asarray(rows(forward, 4)), jnp.asarray(rows(inverse, 4))


def enter(n, me, bat):
    barrier = pltpu.get_barrier_semaphore()

    def greet(k, carry):
        pl.semaphore_signal(
            barrier, inc=1, device_id={"slab": lax.rem(me + k, n)}, device_id_type=MESH
        )
        return carry

    lax.fori_loop(1, n, greet, 0)
    pl.semaphore_signal(barrier, inc=1, device_id={"batch": 1 - bat}, device_id_type=MESH)
    pl.semaphore_wait(barrier, n)


def peer_copy(n, me, k, source, target, landed, sems):
    to = lax.rem(me + k, n)
    return pltpu.make_async_remote_copy(
        src_ref=source(to),
        dst_ref=target(landed),
        send_sem=sems.at[0, k],
        recv_sem=sems.at[1, k],
        device_id={"slab": to},
        device_id_type=MESH,
    )


def send_all(n, me, source, target, sems):
    def step(i, carry):
        k = n // 2 + (i + 1) // 2 * (2 * (i % 2) - 1)
        peer_copy(n, me, k, source, target, me, sems).start()
        return carry

    lax.fori_loop(0, n - 1, step, 0)


def wait_landed(n, me, source, target, sems):
    def step(k, carry):
        peer_copy(n, me, k, source, target, lax.rem(me - k + n, n), sems).wait_recv()
        return carry

    lax.fori_loop(1, n, step, 0)


def wait_sent(n, me, source, target, sems):
    def step(k, carry):
        peer_copy(n, me, k, source, target, me, sems).wait_send()
        return carry

    lax.fori_loop(1, n, step, 0)


def part_count(lanes):
    return min(1, lanes // 128)


def in_parts(source, target, sems):
    parts = part_count(source.shape[2])
    lanes = source.shape[2] // parts
    return [
        (
            lambda to, at=pl.ds(h * lanes, lanes): source.at[to, :, at],
            lambda slot, at=pl.ds(h * lanes, lanes): target.at[slot, :, at],
            sems.at[h],
        )
        for h in range(parts)
    ]


def block_pairs(count):
    return min(PB, count // part_count(count * 16))


def block_lanes(block, pairs):
    return pl.ds(pl.multiple_of(block * (pairs * 16), 128), pairs * 16)


def four(values):
    return jnp.concatenate([values] * 4, axis=-1)


def expand(planes_ref, slot, block, pairs, table_ref):
    rows = planes_ref.shape[1] * planes_ref.shape[2]
    part = planes_ref[slot, :, :, block_lanes(block, pairs)].reshape(rows, pairs * 16)
    both = lax.dot_general(
        part, table_ref[...], (((0,), (0,)), ((), ())), preferred_element_type=F32
    )
    half = both.shape[1] // 2
    return (
        both[:, :half].reshape(pairs, 16, half),
        both[:, half:].reshape(pairs, 16, half),
    )


def own_mask(channels):
    shape = (channels, channels * MX)
    row = lax.broadcasted_iota(jnp.int32, shape, 0)
    col = lax.broadcasted_iota(jnp.int32, shape, 1)
    low = row * MX
    return jnp.where((col >= low) & (col < low + MX), 1.0, 0.0).astype(F32)


def lane_fold(values):
    quarter = values.shape[-1] // 4
    return (
        values[..., :quarter]
        + values[..., quarter : 2 * quarter]
        + values[..., 2 * quarter : 3 * quarter]
        + values[..., 3 * quarter :]
    )


def contract(first, second, table_ref, out_ref, block, pairs):
    both = jnp.concatenate([lane_fold(first), lane_fold(second)], axis=-1)
    both = both.reshape(pairs * 16, both.shape[-1]).astype(BF)
    result = lax.dot_general(
        table_ref[...], both, (((1,), (1,)), ((), ())), preferred_element_type=F32
    )
    out_ref[:, :, block_lanes(block, pairs)] = result.astype(BF).reshape(
        out_ref.shape[0], out_ref.shape[1], pairs * 16
    )


def pair_places(count, block, pairs):
    wide = max(count // MZ, 1)
    deep = count // wide
    step = pairs // wide
    return [m * deep + block * step + k for k in range(step) for m in range(wide)]


def weight_pair(w_ref, block, pairs):
    places = pair_places(w_ref.shape[0], block, pairs)
    return tuple(
        jnp.stack([w_ref[at, part].astype(F32) for at in places], axis=0) for part in range(2)
    )


def mix_forward(n, scale, s1, w, t, ti, r1, r2, s2, sems, pair):
    me = lax.axis_index("slab")
    bat = lax.axis_index("batch")
    enter(n, me, bat)
    one = in_parts(s1, r1.at[bat], sems.at[0])
    two = in_parts(s2, r2, sems.at[1])
    pairs = block_pairs(w.shape[0])
    blocks = w.shape[0] // pairs // len(one)
    for each in one:
        send_all(n, me, *each)
    r1[bat, me] = s1[me]
    cross = pltpu.make_async_remote_copy(
        src_ref=r1.at[bat],
        dst_ref=r1.at[bat],
        send_sem=pair.at[0],
        recv_sem=pair.at[1],
        device_id={"batch": 1 - bat},
        device_id_type=MESH,
    )
    mask = own_mask(16)[None]

    def step(block, carry):
        u0, u1 = expand(r1, bat, block, pairs, t)
        u0, u1 = four(u0 * scale), four(u1 * scale)
        w0, w1 = weight_pair(w, block, pairs)
        v0 = jnp.sum(u0 * w0 - u1 * w1, axis=1, keepdims=True) * mask
        v1 = jnp.sum(u0 * w1 + u1 * w0, axis=1, keepdims=True) * mask
        contract(v0, v1, ti, s2, block, pairs)
        return carry

    for h in range(len(one)):
        wait_landed(n, me, *one[h])
        if h == len(one) - 1:
            cross.start()
        lax.fori_loop(h * blocks, (h + 1) * blocks, step, 0)
        send_all(n, me, *two[h])
    r2[me] = s2[me]
    cross.wait()
    for each in one:
        wait_sent(n, me, *each)
    for each in two:
        wait_landed(n, me, *each)
        wait_sent(n, me, *each)


def mix_backward(
    n, scale_f, scale_i, scale_w, s3, part, w, t, ti, r1, grad, r4, total,
    r3, s4, slots, half, sems, pair,
):
    me = lax.axis_index("slab")
    bat = lax.axis_index("batch")
    enter(n, me, bat)
    one = in_parts(s3, r3.at[bat], sems.at[0])
    two = in_parts(s4, r4, sems.at[1])
    small = (lambda to: part, lambda at: slots.at[at], sems.at[2, 0])
    pairs = block_pairs(w.shape[0])
    blocks = w.shape[0] // pairs // len(one)
    for each in one:
        send_all(n, me, *each)
    send_all(n, me, *small)
    r3[bat, me] = s3[me]
    slots[me] = part[...]

    def across(source, target, at):
        return pltpu.make_async_remote_copy(
            src_ref=source,
            dst_ref=target,
            send_sem=pair.at[2 * at],
            recv_sem=pair.at[2 * at + 1],
            device_id={"batch": 1 - bat},
            device_id_type=MESH,
        )

    cross = across(r3.at[bat], r3.at[bat], 0)
    mask = own_mask(16)[None]

    def gradient(slot, block):
        d0, d1 = expand(r3, slot, block, pairs, t)
        d0, d1 = four(d0), four(d1)
        d0 = jnp.sum(d0 * mask, axis=1, keepdims=True) * scale_i
        d1 = jnp.sum(d1 * mask, axis=1, keepdims=True) * scale_i
        return d0, d1

    def step(block, carry):
        d0, d1 = gradient(bat, block)
        w0, w1 = weight_pair(w, block, pairs)
        contract(d0 * w0 + d1 * w1, d1 * w0 - d0 * w1, ti, s4, block, pairs)
        return carry

    for h in range(len(one)):
        wait_landed(n, me, *one[h])
        if h == len(one) - 1:
            cross.start()
        lax.fori_loop(h * blocks, (h + 1) * blocks, step, 0)
        send_all(n, me, *two[h])
    r4[me] = s4[me]
    wait_landed(n, me, *small)
    wait_sent(n, me, *small)
    summed = slots[0]
    for at in range(1, n):
        summed = summed + slots[at]
    half[bat] = summed
    other = across(half.at[bat], half.at[bat], 1)
    other.start()
    cross.wait()

    def outer(block, carry):
        places = pair_places(w.shape[0], block, pairs)
        first = None
        for slot in range(2):
            u0, u1 = expand(r1, slot, block, pairs, t)
            u0, u1 = four(u0), four(u1)
            d0, d1 = gradient(slot, block)
            d0, d1 = d0 * (scale_f * scale_w), d1 * (scale_f * scale_w)
            real = u0 * d0 + u1 * d1
            imag = u0 * d1 - u1 * d0
            if first is None:
                first = (real, imag)
            else:
                real, imag = first[0] + real, first[1] + imag
                for row, at in enumerate(places):
                    grad[at, 0] = real[row]
                    grad[at, 1] = imag[row]
        return carry

    lax.fori_loop(0, len(one) * blocks, outer, 0)
    other.wait()
    total[...] = half[0] + half[1]
    for each in one:
        wait_sent(n, me, *each)
    for each in two:
        wait_landed(n, me, *each)
        wait_sent(n, me, *each)


def run_forward(n, scale, s1, w, t, ti):
    shape = jax.ShapeDtypeStruct
    return pl.pallas_call(
        functools.partial(mix_forward, n, scale),
        out_shape=(shape((2,) + s1.shape, BF), shape(s1.shape, BF)),
        in_specs=[VMEM] * 4,
        out_specs=(VMEM, VMEM),
        scratch_shapes=[
            pltpu.VMEM(s1.shape, BF),
            pltpu.SemaphoreType.DMA((2, 4, 2, n)),
            pltpu.SemaphoreType.DMA((2,)),
        ],
        compiler_params=pltpu.CompilerParams(
            collective_id=0, has_side_effects=True, vmem_limit_bytes=40 << 20
        ),
        name="mix_forward",
    )(s1, w, t, ti)


def run_backward(n, scales, s3, part, w, t, ti, r1):
    shape = jax.ShapeDtypeStruct
    return pl.pallas_call(
        functools.partial(mix_backward, n, *scales),
        out_shape=(shape(w.shape, F32), shape(s3.shape, BF), shape(part.shape, F32)),
        in_specs=[VMEM] * 6,
        out_specs=(VMEM, VMEM, VMEM),
        scratch_shapes=[
            pltpu.VMEM((2,) + s3.shape, BF),
            pltpu.VMEM(s3.shape, BF),
            pltpu.VMEM((n,) + part.shape, F32),
            pltpu.VMEM((2,) + part.shape, F32),
            pltpu.SemaphoreType.DMA((3, 4, 2, n)),
            pltpu.SemaphoreType.DMA((4,)),
        ],
        compiler_params=pltpu.CompilerParams(
            collective_id=1, has_side_effects=True, vmem_limit_bytes=48 << 20
        ),
        name="mix_backward",
    )(s3, part, w, t, ti, r1)


def plane_tables(rows_y, rows_z):
    phase_y = np_phase(np.arange(rows_y), np_freqs(MY, rows_y), rows_y)
    phase_z = np_phase(np.arange(rows_z), np.arange(MZ), rows_z)
    cy, sy, cz, sz = np.cos(phase_y), np.sin(phase_y), np.cos(phase_z), np.sin(phase_z)
    forward_y = np.concatenate([cy, -sy], axis=1).T
    inverse_y = np.concatenate([cy, -sy], axis=1)
    forward_z = np.stack([np.stack([cz, -sz], axis=1), np.stack([sz, cz], axis=1)], axis=0)
    forward_z = forward_z.transpose(3, 2, 0, 1).reshape(2 * MZ, 2 * rows_z)
    cz, sz = cz.T, sz.T
    inverse_z = np.stack([np.stack([cz, sz], axis=1), np.stack([-sz, cz], axis=1)], axis=0)
    inverse_z = inverse_z.transpose(1, 0, 2, 3).reshape(2 * MZ, 2 * rows_z)
    rows = np.concatenate([forward_y, forward_z, inverse_z], axis=0)
    return [jnp.asarray(v.astype(ml_dtypes.bfloat16)) for v in (rows, inverse_y)]


def table_rows(tables):
    size = tables.shape[0] // 3
    return [tables[k * size : (k + 1) * size] for k in range(3)]


def piece_layout(n):
    count = MY * MZ // n
    wide = max(count // MZ, 1)
    deep = count // wide
    return wide, deep, wide * 16


def pack_planes(acc, kbuf, out):
    planes, n = acc.shape[0], out.shape[0]
    wide, deep, width = piece_layout(n)
    for x in range(planes):
        for g in range(kbuf.shape[0]):
            kbuf[g, pl.ds(x, 2 * MZ, stride=planes), :] = acc[x, :, g * 128 : (g + 1) * 128]
    group = 128 // width
    for j in range(n):
        m0 = j * wide * deep // MZ
        k0 = j * wide * deep % MZ if wide == 1 else 0
        for first in range(0, deep, group):
            parts = [
                kbuf[
                    m0 * 16 // 128,
                    (k0 + first + q) * 2 * planes : (k0 + first + q + 1) * 2 * planes,
                    m0 * 16 % 128 : m0 * 16 % 128 + width,
                ]
                for q in range(group)
            ]
            out[j, :, first * width : first * width + 128] = jnp.concatenate(
                parts, axis=1
            ).astype(BF)


def unpack_planes(received, kbuf, staged):
    planes, n = staged.shape[0], received.shape[0]
    wide, deep, width = piece_layout(n)
    group = 128 // width
    for k in range(MZ):
        owners = [j for j in range(n) if wide > 1 or j % (MZ // deep) == k // deep]
        lane = (k % deep) * width
        low = lane // 128 * 128
        for first in range(0, len(owners), group):
            parts = [
                received[j, :, low : low + 128].astype(F32)[:, lane - low : lane - low + width]
                for j in owners[first : first + group]
            ]
            kbuf[first // group, k * 2 * planes : (k + 1) * 2 * planes, :] = jnp.concatenate(
                parts, axis=1
            )
    for x in range(planes):
        for g in range(kbuf.shape[0]):
            staged[x, :, g * 128 : (g + 1) * 128] = kbuf[
                g, pl.ds(x, 2 * MZ, stride=planes), :
            ].astype(BF)


def plane_forward(source, fy, fz, lines, acc, x):
    channels = source.shape[0]
    rows = 2 * MY
    for c in range(0, channels, 2):
        couple = jnp.concatenate([source[c, 0], source[c + 1, 0]], axis=1)
        result = jnp.dot(fy, couple, preferred_element_type=F32)
        half = result.shape[1] // 2
        lines[pl.ds(c, rows, stride=channels), :] = result[:, :half]
        lines[pl.ds(c + 1, rows, stride=channels), :] = result[:, half:]
    half = MY * channels
    both = jnp.concatenate([lines[:half].astype(BF), lines[half:].astype(BF)], axis=1)
    acc[x] = lax.dot_general(fz, both, (((1,), (1,)), ((), ())), preferred_element_type=F32)


def spread_map(weight, spread, turned):
    size = spread.shape[0]
    place = lax.broadcasted_iota(jnp.int32, (size, weight.shape[0]), 0) >> 4
    lane = lax.broadcasted_iota(jnp.int32, (size, weight.shape[0]), 1)
    copies = jnp.where(place == lane, 1.0, 0.0).astype(BF)
    contracted = 0 if turned else 1
    rows = lax.dot_general(
        copies, weight[...], (((1,), (contracted,)), ((), ())), preferred_element_type=F32
    ).astype(BF)
    full = lax.dot_general(rows, copies, (((1,), (1,)), ((), ())), preferred_element_type=F32)
    row = lax.broadcasted_iota(jnp.int32, (size, size), 0)
    col = lax.broadcasted_iota(jnp.int32, (size, size), 1)
    spread[...] = jnp.where((row & 15) == (col & 15), full, 0.0).astype(BF)


def plane_inverse(staged, iz, iy, factor, lines, pre, x):
    channels = pre.shape[0]
    half = MY * channels
    rolled = factor * lax.dot_general(
        staged[x], iz, (((0,), (0,)), ((), ())), preferred_element_type=F32
    )
    lines[:half] = rolled[:, : rolled.shape[1] // 2]
    lines[half:] = rolled[:, rolled.shape[1] // 2 :]
    for c in range(0, channels, 2):
        pieces = []
        for at in (c, c + 1):
            pieces.append(lines[pl.ds(at, 2 * MY, stride=channels), :].astype(BF))
        result = jnp.dot(
            iy[...], jnp.concatenate(pieces, axis=1), preferred_element_type=F32
        )
        pre[c] = result[:, : result.shape[1] // 2]
        pre[c + 1] = result[:, result.shape[1] // 2 :]


def field_forward(field, tables, out, lines, acc, kbuf):
    x = pl.program_id(0)
    fy, fz, _ = table_rows(tables)
    plane_forward(field, fy, fz, lines, acc, x)

    @pl.when(x == pl.num_programs(0) - 1)
    def _():
        pack_planes(acc, kbuf, out)


def tile_rows(ref, step):
    parts = []
    for half in range(2):
        at = slice((2 * step + half) * 16, (2 * step + half + 1) * 16)
        value = ref[:, 0, at, :]
        parts.append(value.reshape(value.shape[0] * 16, value.shape[2]))
    return jnp.concatenate(parts, axis=1)


GELU_K = math.sqrt(2.0 / math.pi)
GELU_C = 0.044715


def gelu_slope(value):
    square = value * value
    bent = jnp.tanh(value * (GELU_K + (GELU_K * GELU_C) * square))
    side = value * (0.5 * GELU_K + (1.5 * GELU_K * GELU_C) * square)
    return (1.0 + bent) * (0.5 + (1.0 - bent) * side)


def middle(
    factor, received, field, cot, weight, bias, tables, iy,
    dpre, out, part, lines, acc, kbuf, staged, pre, spread, outer, sums, shift,
):
    x = pl.program_id(0)
    fy, fz, iz = table_rows(tables)
    channels = field.shape[0]

    @pl.when(x == 0)
    def _():
        unpack_planes(received, kbuf, staged)
        spread_map(weight, spread, False)
        row = lax.broadcasted_iota(jnp.int32, (channels, channels), 0)
        col = lax.broadcasted_iota(jnp.int32, (channels, channels), 1)
        column = jnp.sum(jnp.where(row == col, bias[...], 0.0), axis=1, keepdims=True)
        shift[...] = jnp.broadcast_to(column, shift.shape)
        outer[...] = jnp.zeros_like(outer)
        sums[...] = jnp.zeros_like(sums)

    plane_inverse(staged, iz, iy, factor, lines, pre, x)

    for at in range(field.shape[2] // 32):
        tile = tile_rows(field, at)
        mixed = jnp.dot(spread[...], tile, preferred_element_type=F32)
        width = mixed.shape[1] // 2
        halves = []
        for half in range(2):
            rows = slice((2 * at + half) * 16, (2 * at + half + 1) * 16)
            value = mixed[:, half * width : (half + 1) * width].reshape(channels, 16, width)
            value = value + pre[:, rows, :] + shift[...][:, None, :]
            slope = gelu_slope(value) * cot[:, 0, rows, :].astype(F32)
            rounded = slope.astype(BF)
            dpre[:, 0, rows, :] = rounded
            wide = rounded.astype(F32)
            sums[...] += wide[:, :8] + wide[:, 8:]
            halves.append(rounded.reshape(channels * 16, width))
        outer[...] += lax.dot_general(
            tile, jnp.concatenate(halves, axis=1), (((1,), (1,)), ((), ())),
            preferred_element_type=F32,
        )
    plane_forward(dpre, fy, fz, lines, acc, x)

    @pl.when(x == pl.num_programs(0) - 1)
    def _():
        pack_planes(acc, kbuf, out)
        size = channels * 16
        row = lax.broadcasted_iota(jnp.int32, (size, size), 0)
        col = lax.broadcasted_iota(jnp.int32, (size, size), 1)
        kept = jnp.where((row & 15) == (col & 15), outer[...], 0.0)
        kept = jnp.sum(kept.reshape(channels, 16, size), axis=1)
        place = lax.broadcasted_iota(jnp.int32, (size, 128), 0) >> 4
        lane = lax.broadcasted_iota(jnp.int32, (size, 128), 1)
        gather = jnp.where(place == lane, 1.0, 0.0).astype(F32)
        part[:channels] = jnp.dot(
            kept, gather, preferred_element_type=F32, precision=lax.Precision.HIGHEST
        )
        part[channels:] = jnp.sum(sums[...], axis=1)


def last(factor, received, dpre, weight, tables, iy, grad, lines, kbuf, staged, pre, spread):
    x = pl.program_id(0)
    iz = table_rows(tables)[2]
    channels = dpre.shape[0]

    @pl.when(x == 0)
    def _():
        unpack_planes(received, kbuf, staged)
        spread_map(weight, spread, True)

    plane_inverse(staged, iz, iy, factor, lines, pre, x)

    for at in range(dpre.shape[2] // 32):
        mixed = jnp.dot(spread[...], tile_rows(dpre, at), preferred_element_type=F32)
        width = mixed.shape[1] // 2
        for half in range(2):
            rows = slice((2 * at + half) * 16, (2 * at + half + 1) * 16)
            value = mixed[:, half * width : (half + 1) * width].reshape(channels, 16, width)
            grad[:, 0, rows, :] = (value + pre[:, rows, :]).astype(BF)


def whole(array):
    zeros = (0,) * array.ndim
    return pl.BlockSpec(array.shape, lambda x: zeros)


def plane_block(array):
    c, _, y, z = array.shape
    return pl.BlockSpec((c, 1, y, z), lambda x: (0, x, 0, 0))


def scratch(field, *names):
    c, planes, y, z = field.shape
    every = {
        "lines": pltpu.VMEM((2 * MY * c, z), F32),
        "acc": pltpu.VMEM((planes, 2 * MZ, MY * c), F32),
        "kbuf": pltpu.VMEM((MY * c // 128, 2 * MZ * planes, 128), F32),
        "staged": pltpu.VMEM((planes, 2 * MZ, MY * c), BF),
        "pre": pltpu.VMEM((c, y, z), F32),
        "spread": pltpu.VMEM((16 * c, 16 * c), BF),
        "outer": pltpu.VMEM((16 * c, 16 * c), F32),
        "shift": pltpu.VMEM((c, z), F32),
        "sums": pltpu.VMEM((c, 8, z), F32),
    }
    return [every[name] for name in names]


def params():
    return pltpu.CompilerParams(vmem_limit_bytes=48 << 20)


def run_first(n, field, tables):
    c, planes, _, _ = field.shape
    out = jax.ShapeDtypeStruct((n, 2 * planes, MY * MZ // n * c), BF)
    return pl.pallas_call(
        field_forward,
        grid=(planes,),
        out_shape=out,
        in_specs=[plane_block(field), whole(tables)],
        out_specs=whole(out),
        scratch_shapes=scratch(field, "lines", "acc", "kbuf"),
        compiler_params=params(),
        name="field_forward",
    )(field, tables)


def run_middle(factor, received, field, cot, weight, bias, tables, iy):
    c, planes, _, _ = field.shape
    out = jax.ShapeDtypeStruct(received.shape, BF)
    part = jax.ShapeDtypeStruct((2 * c, 128), F32)
    flat = [weight, bias, tables, iy]
    return pl.pallas_call(
        functools.partial(middle, factor),
        grid=(planes,),
        out_shape=(jax.ShapeDtypeStruct(field.shape, BF), out, part),
        in_specs=[whole(received), plane_block(field), plane_block(cot)] + [whole(v) for v in flat],
        out_specs=(plane_block(field), whole(out), whole(part)),
        scratch_shapes=scratch(
            field, "lines", "acc", "kbuf", "staged", "pre", "spread", "outer", "sums", "shift"
        ),
        compiler_params=params(),
        name="middle",
    )(received, field, cot, *flat)


def run_last(factor, received, dpre, weight, tables, iy):
    c, planes, _, _ = dpre.shape
    flat = [weight, tables, iy]
    return pl.pallas_call(
        functools.partial(last, factor),
        grid=(planes,),
        out_shape=jax.ShapeDtypeStruct(dpre.shape, BF),
        in_specs=[whole(received), plane_block(dpre)] + [whole(v) for v in flat],
        out_specs=plane_block(dpre),
        scratch_shapes=scratch(dpre, "lines", "kbuf", "staged", "pre", "spread"),
        compiler_params=params(),
        name="last",
    )(received, dpre, *flat)


def body(field, cotangent, spectral_weight, point_weight, point_bias):
    samples, channels, planes, rows_y, rows_z = field.shape
    n = lax.axis_size("slab")
    total_samples = samples * lax.axis_size("batch")
    cells = n * planes * rows_y * rows_z
    scale_f = 1.0 / math.sqrt(cells)
    scale_i = 1.0 / math.sqrt(MX * MY * MZ)
    scale_p = 1.0 / math.sqrt(total_samples * cells)
    scale_w = math.sqrt(MX * MY * MZ / (total_samples * cells))
    tables, iy = plane_tables(rows_y, rows_z)
    t, ti = x_tables(n, planes)
    f = field.reshape(field.shape[1:])
    cot = cotangent.reshape(cotangent.shape[1:])
    s1 = run_first(n, f, tables)
    r1, r2 = run_forward(n, scale_f, s1, spectral_weight, t, ti)
    bias = point_bias[None, :]
    dpre, s3, part = run_middle(
        scale_i, r2, f, cot, point_weight, bias, tables, iy
    )
    grad_spec, r4, total = run_backward(
        n, (scale_f, scale_i, scale_w), s3, part, spectral_weight, t, ti, r1
    )
    input_grad = run_last(scale_f, r4, dpre, point_weight, tables, iy)
    return (
        input_grad[None],
        grad_spec,
        scale_p * total[:channels, :channels],
        scale_p * jnp.sum(total[channels:], axis=1),
    )


def solution(mesh):
    placed = (
        P("batch", None, "slab", None, None),
        P("batch", None, "slab", None, None),
        P("slab", None, None, None),
        P(),
        P(),
    )
    return jax.shard_map(
        body,
        mesh=mesh,
        in_specs=placed,
        out_specs=(P("batch", None, "slab", None, None), P("slab", None, None, None), P(), P()),
        check_vma=False,
    )
```
